256 devices in a mesh: cfg: 2 (over x_hi), blk: 16 (over z, core), uly: 8 (over x_lo, y).
Axes of the slice: x: 4 (x_hi: 2, x_lo: 2; x = x_hi * 2 + x_lo), y: 4, z: 8, core: 2. Of those that a mesh axis runs over, the one named last changes fastest.
Arguments:
- queries: bfloat16 [32768, 3072], P(('cfg', 'blk', 'uly')), parts along dimension 0, may hold values from -6 to 6
- key_states: bfloat16 [32768, 3072], P(('cfg', 'blk', 'uly')), parts along dimension 0, may hold values from -6 to 6
- value_states: bfloat16 [32768, 3072], P(('cfg', 'blk', 'uly')), parts along dimension 0, may hold values from -6 to 6
- query_gain: float32 [128], replicated, may hold values from 0.1 to 1.9
- key_gain: float32 [128], replicated, may hold values from 0.1 to 1.9
- neighbors: int32 [256, 27], P('blk'), may hold values from 0 to 255, as said below
- counts: int32 [256], P('blk'), may hold values from 1 to 27, as said below
Outputs:
- attended: bfloat16 [32768, 3072], P(('cfg', 'blk', 'uly')), parts along dimension 0
The draws below stay inside these ranges and needn't reach their ends.
There are 2 independent parts, one for each index of `cfg`. The reference program is written for one: setup_inputs(seed, part) draws one part's arguments, and reference() takes and returns one part's arrays. A program takes and returns all parts, laid end to end along the dimension named above; an argument that names none is the same for every part. Nothing has to cross between parts.
Inputs may be any that keep to these rules, and one draw needn't show every extreme that they name: `neighbors`: tiles are numbered frame by frame on a grid of 3 x 20 tiles a frame (number = frame 3 * 20 + row 20 + column; the last frame may be partial). The first counts[i] entries of row i are distinct tiles of the 3 x 3 x 3 block of tiles around tile i, tile i among them; the other entries equal i. Every entry differs from i by at most 81, and that distance is reached. `counts`: number of live entries at the head of each row of neighbors.
All inputs are finite; a program needn't handle non-finite values.
Results may differ from the reference program's by a relative error of at most 0.0078.
Values may be sent and summed in bfloat16 or wider, within the bound.
A program may use at most 128 MiB of HBM per device.

```python
import jax
import jax.numpy as jnp
from jax import lax

D = 3072
HEADS = 24
HD = 128
TOKENS = 16384
HT = 3
WT = 20
NB = 27
TILES = 256


def tile_window(key):
    frame = HT * WT
    tile_ids = jnp.arange(TILES, dtype=jnp.int32)
    frame_pos = tile_ids // frame
    row_pos = tile_ids // WT % HT
    column_pos = tile_ids % WT
    offset_ids = jnp.arange(27, dtype=jnp.int32)
    step_t = offset_ids // 9 - 1
    step_h = offset_ids // 3 % 3 - 1
    step_w = offset_ids % 3 - 1
    near_t = frame_pos[:, None] + step_t[None, :]
    near_h = row_pos[:, None] + step_h[None, :]
    near_w = column_pos[:, None] + step_w[None, :]
    candidate = near_t * frame + near_h * WT + near_w
    inside = (near_h >= 0) & (near_h < HT) & (near_w >= 0) & (near_w < WT) & (candidate >= 0) & (candidate < TILES)
    keys_split = jax.random.split(key, 5)
    keep_bits = jax.random.randint(keys_split[0], (TILES, 27), 0, 4) > 0
    forced_t = jax.random.randint(keys_split[1], (), 0, TILES // frame - 1)
    forced_h = jax.random.randint(keys_split[2], (), 1, HT - 1)
    forced_w = jax.random.randint(keys_split[3], (), 1, WT - 1)
    forced = tile_ids == forced_t * frame + forced_h * WT + forced_w
    is_center = offset_ids == 13
    live_slot = inside & (keep_bits | is_center[None, :] | forced[:, None])
    ranking = jax.random.randint(keys_split[4], (TILES, 27), 0, 2 ** 20) * 32 + offset_ids[None, :]
    sort_key = jnp.where(live_slot, ranking, 2 ** 30 + offset_ids[None, :])
    order_ids = jnp.argsort(sort_key, axis=1, stable=True)
    sorted_tiles = jnp.take_along_axis(candidate, order_ids, axis=1)
    sorted_live = jnp.take_along_axis(live_slot, order_ids, axis=1)
    padded = jnp.where(sorted_live, sorted_tiles, tile_ids[:, None]).astype(jnp.int32)
    live_count = jnp.sum(live_slot.astype(jnp.int32), axis=1).astype(jnp.int32)
    return (padded, live_count)


def draw_neighbors(key, part):
    padded, live_count = tile_window(key)
    return padded


def draw_counts(key, part):
    padded, live_count = tile_window(key)
    return live_count


def block_scale(stream_key, extent, cuts, smallest, largest):
    level = 1.0
    for dim, shards_of in cuts:
        steps = jax.random.uniform(jax.random.fold_in(jax.random.fold_in(stream_key, 6), dim), (shards_of,), jnp.float32, smallest / len(cuts), largest / len(cuts))
        level = level * jnp.repeat(jnp.exp(steps), extent[dim] // shards_of).reshape((-1,) + (1,) * (len(extent) - 1 - dim))
    return level


def gaussian(own_key, extent, spread, reach, pieces=(), held_as=jnp.bfloat16):
    values = jax.random.normal(own_key, extent, jnp.float32) * spread
    if len(pieces) > 0:
        values = block_scale(own_key, extent, pieces, -0.22, 0.18) * values
    return jnp.clip(values, min=-reach, max=reach).astype(held_as)


def setup_inputs(seed: int = 0, part: int = 0) -> dict:
    keys = jax.random.split(jax.random.key(seed), 8)
    own_keys = jax.random.split(jax.random.fold_in(keys[7], part), 8)
    queries = gaussian(own_keys[0], (TOKENS, D), 1.0, 6.0, ((0, 128),))
    key_states = gaussian(own_keys[1], (TOKENS, D), 1.0, 6.0, ((0, 128),))
    value_states = gaussian(own_keys[2], (TOKENS, D), 1.0, 6.0, ((0, 128),))
    query_gain = jnp.clip(1.0 + 0.18 * jax.random.normal(keys[3], (HD,), jnp.float32), 0.1, 1.9)
    key_gain = jnp.clip(1.0 + 0.18 * jax.random.normal(keys[4], (HD,), jnp.float32), 0.1, 1.9)
    neighbors = draw_neighbors(jax.random.fold_in(keys[7], 71), part)
    counts = draw_counts(jax.random.fold_in(keys[7], 71), part)
    return dict(queries=queries, key_states=key_states, value_states=value_states, query_gain=query_gain, key_gain=key_gain, neighbors=neighbors, counts=counts)


def normalize(states, gain):
    widened = states.astype(jnp.float32)
    factor = lax.rsqrt(lax.optimization_barrier(jnp.mean(widened * widened, axis=-1, keepdims=True)) + 1e-06)
    return (widened * factor * gain).astype(jnp.bfloat16)

def attend_group(query_tiles, key_tiles, value_tiles, neighbor_rows, count_rows):
    near_keys = key_tiles[neighbor_rows].astype(jnp.float32)
    near_values = value_tiles[neighbor_rows].astype(jnp.float32)
    factor = query_tiles.shape[-1] ** (-0.5)
    scores = jnp.einsum('bihe,bnjhe->bhinj', query_tiles.astype(jnp.float32), near_keys) * factor
    slot_ids = jnp.arange(neighbor_rows.shape[1], dtype=jnp.int32)
    live_slot = slot_ids[None, :] < count_rows[:, None]
    weights = jnp.where(live_slot[:, None, None, :, None], jnp.exp(scores), jnp.float32(0.0))
    totals = lax.optimization_barrier(jnp.sum(weights, axis=(3, 4), keepdims=True))
    shares = (weights / totals).astype(jnp.bfloat16)
    mixed = jnp.einsum('bhinj,bnjhe->bihe', shares.astype(jnp.float32), near_values)
    return mixed.astype(jnp.bfloat16)

def reference(queries, key_states, value_states, query_gain, key_gain, neighbors, counts):
    normed_q = normalize(queries.reshape(TILES, 64, HEADS, HD), query_gain)
    normed_k = normalize(key_states.reshape(TILES, 64, HEADS, HD), key_gain)
    value_tiles = value_states.reshape(TILES, 64, HEADS, HD)

    def one_group(items):
        return attend_group(items[0], normed_k, value_tiles, items[1], items[2])
    result = lax.map(one_group, (normed_q.reshape(TILES // 8, 8, 64, HEADS, HD), neighbors.reshape(TILES // 8, 8, NB), counts.reshape(TILES // 8, 8)))
    return result.reshape(TILES * 64, HEADS * HD)
```

```python
import functools
import math

import jax
import jax.numpy as jnp
from jax import lax
from jax.experimental import pallas as pl
from jax.experimental.pallas import tpu as pltpu
from jax.sharding import PartitionSpec as P

MESH = pl.DeviceIdType.MESH
TILE = 64
WIDE = 20
FRAME = 60
REACH = 6
GROUP = 2
SPAN = (GROUP + 2) * TILE
CENTRES = tuple(FRAME * t + WIDE * h for t in (-1, 0, 1) for h in (-1, 0, 1))
NEAR = (3, 4, 5)
MIDDLE = (1, 2, 6, 7)
FAR = (0, 8)


def kernel(
    blocks, peers, heads,
    neighbors, counts, queries, keys, values, query_gain, key_gain,
    out,
    kv, queries_in, keys_out, queries_out, total, acc, mask, mixed,
    uly_send, uly_recv, ring_send, ring_recv, pair_send, pair_recv, back_send, back_recv,
):
    tokens = queries.shape[0]
    hd = query_gain.shape[1]
    block = tokens * peers
    tiles = block // TILE
    cfg, me, mine = lax.axis_index("cfg"), lax.axis_index("blk"), lax.axis_index("uly")
    core = lax.rem(me, 2)
    above, below = lax.rem(me + 2, blocks), lax.rem(me + blocks - 2, blocks)
    pair = me + 1 - 2 * core
    scale = hd ** -0.5 * math.log2(math.e)

    def at_blk(b):
        return (cfg, b, mine)

    def at_uly(u):
        return (cfg, me, u)

    def partner(d):
        return lax.rem(mine + d, peers)

    barrier = pltpu.get_barrier_semaphore()
    for b in (above, below, pair):
        pl.semaphore_signal(barrier, inc=1, device_id=at_blk(b), device_id_type=MESH)
    for d in range(1, peers):
        pl.semaphore_signal(barrier, inc=1, device_id=at_uly(partner(d)), device_id_type=MESH)
    pl.semaphore_wait(barrier, 3 + peers - 1)

    own = REACH * block

    def columns(u, h):
        return pl.ds(pl.multiple_of((u * heads + h) * hd, hd), hd)

    def my_rows(start):
        return pl.ds(pl.multiple_of(start + mine * tokens, tokens), tokens)

    def normed(states, gain, u, h):
        wide = states[:, columns(u, h)].astype(jnp.float32)
        factor = lax.rsqrt(jnp.mean(wide * wide, axis=-1, keepdims=True) + 1e-06)
        return (wide * factor * gain[...]).astype(jnp.bfloat16)

    def spread(kind, h):
        if kind == 2:
            landing = queries_in.at[h, my_rows(0), :]
            queries_in[h, my_rows(0), :] = normed(queries, query_gain, mine, h)
        elif kind == 1:
            landing = kv.at[h, 1, my_rows(own), :]
            kv[h, 1, my_rows(own), :] = values[:, columns(mine, h)]
        else:
            landing = kv.at[h, 0, my_rows(own), :]
            kv[h, 0, my_rows(own), :] = normed(keys, key_gain, mine, h)

        def send(d, carry):
            u = partner(d)
            if kind == 2:
                queries_out[h, u] = normed(queries, query_gain, u, h)
                source = queries_out.at[h, u]
            elif kind == 1:
                source = values.at[:, columns(u, h)]
            else:
                keys_out[h, u] = normed(keys, key_gain, u, h)
                source = keys_out.at[h, u]
            pltpu.make_async_remote_copy(
                source, landing, uly_send.at[kind, h], uly_recv.at[kind, h],
                device_id=at_uly(u), device_id_type=MESH,
            ).start()
            return carry

        lax.fori_loop(1, peers, send, 0)

    rest = (peers - 1) * tokens

    def wait_bytes(ref, sem):
        pltpu.make_async_copy(ref, ref, sem).wait()

    def wait_spread(kind, h):
        ref = queries_in.at[h, pl.ds(0, rest), :] if kind == 2 else kv.at[h, kind, pl.ds(own, rest), :]
        wait_bytes(ref, uly_recv.at[kind, h])

    sent = []

    def ring(unit, slot, source, target, rows, to):
        h, which = unit
        copy = pltpu.make_async_remote_copy(
            kv.at[h, which, pl.ds(source, rows), :], kv.at[h, which, pl.ds(target, rows), :],
            ring_send.at[h, which, slot], ring_recv.at[h, which, slot],
            device_id=at_blk(to), device_id_type=MESH,
        )
        copy.start()
        sent.append(copy)
        return copy

    def share(unit, slot, source):
        h, which = unit
        target = pl.multiple_of(source + (2 * core - 1) * block, block)
        copy = pltpu.make_async_remote_copy(
            kv.at[h, which, pl.ds(source, block), :], kv.at[h, which, pl.ds(target, block), :],
            pair_send.at[h, which, slot], pair_recv.at[h, which, slot],
            device_id=at_blk(pair), device_id_type=MESH,
        )
        copy.start()
        sent.append(copy)
        return copy

    units = [(h, which) for h in range(heads) for which in (1, 0)]
    n_units = len(units)
    ringed, shared = {}, {}

    def step(k):
        if k < n_units:
            unit = units[k]
            wait_spread(unit[1], unit[0])
            ringed[k, 0] = ring(unit, 0, own, own - 2 * block, block, above)
            ringed[k, 1] = ring(unit, 1, own, own + 2 * block, block, below)
            shared[k, 0] = share(unit, 0, own)
        n = k - 1
        if 0 <= n < n_units:
            unit = units[n]
            ringed[n, 0].wait_recv()
            ringed[n, 2] = ring(unit, 2, own - 2 * block, own - 4 * block, block, above)
            ringed[n, 1].wait_recv()
            ringed[n, 3] = ring(unit, 3, own + 2 * block, own + 4 * block, block, below)
            shared[n, 1] = share(unit, 1, own - 2 * block)
            shared[n, 2] = share(unit, 2, own + 2 * block)
        n = k - 2
        if 0 <= n < n_units:
            unit = units[n]
            ringed[n, 2].wait_recv()
            ringed[n, 3].wait_recv()
            ringed[n, 4] = ring(
                unit, 4,
                pl.multiple_of(own + (4 - 8 * core) * block, block),
                pl.multiple_of(own + (6 - 12 * core) * block, block),
                block, lax.rem(me + blocks + 4 * core - 2, blocks),
            )
            ringed[n, 5] = ring(
                unit, 5,
                pl.multiple_of(own - 3 * block - TILE + core * (7 * block + TILE), TILE),
                pl.multiple_of(own - 5 * block - TILE + core * (11 * block + TILE), TILE),
                TILE, lax.rem(me + blocks + 2 - 4 * core, blocks),
            )
            shared[n, 3] = share(unit, 3, own - 4 * block)
            shared[n, 4] = share(unit, 4, own + 4 * block)
        n = k - 3
        if 0 <= n < n_units:
            unit = units[n]
            ringed[n, 4].wait_recv()
            ringed[n, 5].wait_recv()
            shared[n, 5] = share(unit, 5, pl.multiple_of(own + (6 - 12 * core) * block, block))

    def build_mask():
        shape = (16, SPAN)
        row = lax.broadcasted_iota(jnp.int32, shape, 0)
        place = lax.broadcasted_iota(jnp.int32, shape, 1) // TILE
        centre = (row // 3 - 1) * FRAME + (row % 3 - 1) * WIDE

        def one(t, carry):
            tile = centre + place + (me * tiles + t - 1 - lax.rem(t, GROUP))
            live = jnp.zeros(shape, jnp.float32)
            count = counts[0, t]
            for n in range(neighbors.shape[1]):
                entry = jnp.where(n < count, neighbors[t, n], -(2 ** 20))
                live = jnp.where(tile == entry, 1.0, live)
            mask[t] = live
            return carry

        lax.fori_loop(0, tiles, one, 0)

    def attend(h, windows, first=False, last=False):
        rows = GROUP * TILE

        def group(g, carry):
            t = g * GROUP
            mine_rows = pl.ds(pl.multiple_of(t * TILE, rows), rows)
            q = queries_in[h, mine_rows, :]
            if first:
                sums = jnp.zeros((rows, 128), jnp.float32)
                result = jnp.zeros((rows, hd), jnp.float32)
            else:
                sums = total[h, mine_rows, :]
                result = acc[h, mine_rows, :]
            for w in windows:
                near = pl.ds(pl.multiple_of(own + (t + CENTRES[w] - 1) * TILE, TILE), SPAN)
                scores = lax.dot_general(
                    q, kv[h, 0, near, :], (((1,), (1,)), ((), ())), preferred_element_type=jnp.float32
                )
                weights = jnp.exp2(scores * scale)
                live = jnp.concatenate(
                    [jnp.broadcast_to(mask[t + a, pl.ds(w, 1), :], (TILE, SPAN)) for a in range(GROUP)], axis=0
                )
                weights = weights * live
                for part in range(0, SPAN, 128):
                    sums = sums + weights[:, part : part + 128]
                result = result + jnp.dot(
                    weights.astype(jnp.bfloat16), kv[h, 1, near, :], preferred_element_type=jnp.float32
                )
            if last:
                mixed[h, mine_rows, :] = (result / jnp.sum(sums, axis=-1, keepdims=True)).astype(jnp.bfloat16)
            else:
                total[h, mine_rows, :] = sums
                acc[h, mine_rows, :] = result
            return carry

        lax.fori_loop(0, tiles // GROUP, group, 0)

    def near_part(h):
        wait_spread(2, h)
        for which in (1, 0):
            n = units.index((h, which))
            for slot in (0, 1, 2):
                shared[n, slot].wait_recv()
        attend(h, NEAR, first=True)

    def middle_part(h):
        for which in (1, 0):
            n = units.index((h, which))
            for slot in (3, 4):
                shared[n, slot].wait_recv()
        attend(h, MIDDLE)

    def far_part(h):
        for which in (1, 0):
            shared[units.index((h, which)), 5].wait_recv()
        attend(h, FAR, last=True)
        landing = out.at[:, columns(mine, h)]

        def send(d, carry):
            u = partner(d)
            pltpu.make_async_remote_copy(
                mixed.at[h, pl.ds(pl.multiple_of(u * tokens, tokens), tokens), :], landing,
                back_send.at[h], back_recv.at[h], device_id=at_uly(u), device_id_type=MESH,
            ).start()
            return carry

        lax.fori_loop(1, peers, send, 0)
        out[:, columns(mine, h)] = mixed[h, my_rows(0), :]

    for h in range(heads):
        spread(1, h)
        spread(0, h)
    for h in range(heads):
        spread(2, h)
    step(0)
    step(1)
    build_mask()
    step(2)
    for k in range(3, n_units + 3):
        step(k)
        if k % 2 == 1:
            h = (k - 3) // 2
            if h >= 1:
                far_part(h - 1)
            near_part(h)
        else:
            middle_part((k - 4) // 2)
    far_part(heads - 1)

    for copy in sent:
        copy.wait_send()
    for h in range(heads):
        for kind in range(3):
            wait_bytes(queries_in.at[h, pl.ds(0, rest), :], uly_send.at[kind, h])
        wait_bytes(queries_in.at[h, pl.ds(0, rest), :], back_send.at[h])
        wait_bytes(queries_in.at[h, pl.ds(0, rest), :], back_recv.at[h])


def solution(mesh):
    blocks, peers = mesh.shape["blk"], mesh.shape["uly"]

    def per_device(queries, keys, values, query_gain, key_gain, neighbors, counts):
        tokens, width = queries.shape
        hd = query_gain.shape[0]
        heads = width // hd // peers
        block = tokens * peers
        tiles = block // TILE
        vmem = pl.BlockSpec(memory_space=pltpu.VMEM)
        smem = pl.BlockSpec(memory_space=pltpu.SMEM)
        dma = pltpu.SemaphoreType.DMA
        return pl.pallas_call(
            functools.partial(kernel, blocks, peers, heads),
            out_shape=jax.ShapeDtypeStruct((tokens, width), jnp.bfloat16),
            in_specs=[smem, smem] + [vmem] * 5,
            out_specs=vmem,
            scratch_shapes=[
                pltpu.VMEM((heads, 2, (2 * REACH + 1) * block, hd), jnp.bfloat16),
                pltpu.VMEM((heads, block, hd), jnp.bfloat16),
                pltpu.VMEM((heads, peers, tokens, hd), jnp.bfloat16),
                pltpu.VMEM((heads, peers, tokens, hd), jnp.bfloat16),
                pltpu.VMEM((heads, block, 128), jnp.float32),
                pltpu.VMEM((heads, block, hd), jnp.float32),
                pltpu.VMEM((tiles, 16, SPAN), jnp.float32),
                pltpu.VMEM((heads, block, hd), jnp.bfloat16),
                dma((3, heads)), dma((3, heads)),
                dma((heads, 2, 6)), dma((heads, 2, 6)),
                dma((heads, 2, 6)), dma((heads, 2, 6)),
                dma((heads,)), dma((heads,)),
            ],
            compiler_params=pltpu.CompilerParams(
                collective_id=0, has_side_effects=True, vmem_limit_bytes=56 * 2 ** 20
            ),
        )(neighbors, counts.reshape(1, -1), queries, keys, values, query_gain.reshape(1, -1), key_gain.reshape(1, -1))

    tokens = P(("cfg", "blk", "uly"), None)
    return jax.shard_map(
        per_device,
        mesh=mesh,
        in_specs=(tokens, tokens, tokens, P(), P(), P("blk", None), P("blk")),
        out_specs=tokens,
        check_vma=False,
    )
```

```python
import functools
import math

import jax
import jax.numpy as jnp
from jax import lax
from jax.experimental import pallas as pl
from jax.experimental.pallas import tpu as pltpu
from jax.sharding import PartitionSpec as P

MESH = pl.DeviceIdType.MESH
TILE = 64
WIDE = 20
FRAME = 60
REACH = 6
GROUP = 2
SPAN = (GROUP + 2) * TILE
CENTRES = tuple(FRAME * t + WIDE * h for t in (-1, 0, 1) for h in (-1, 0, 1))
NEAR = (3, 4, 5)
MIDDLE = (1, 2, 6, 7)
FAR = (0, 8)


PIECES = (1, 5, 4, 4, 2)
LOWER_FIRST = (0, 1, 6, 10, 14)
UPPER_FIRST = (15, 0, 5, 9, 13)
EARLY = 2


def kernel(
    blocks, peers, heads,
    neighbors, counts, queries_hbm, keys_hbm, values_hbm, query_gain, key_gain,
    out,
    queries, keys, values, kv, queries_in, keys_out, queries_out, total, acc, mask, mixed,
    load_sem, uly_send, uly_recv, early_recv, ring_send, ring_recv, pair_send, pair_recv,
    tail_send, tail_recv, tail_pair_send, tail_pair_recv, back_send, back_recv, own_sem,
):
    tokens = queries.shape[0]
    hd = query_gain.shape[1]
    block = tokens * peers
    tiles = block // TILE
    cfg, me, mine = lax.axis_index("cfg"), lax.axis_index("blk"), lax.axis_index("uly")
    core = lax.rem(me, 2)
    above, below = lax.rem(me + 2, blocks), lax.rem(me + blocks - 2, blocks)
    pair = me + 1 - 2 * core
    scale = hd ** -0.5 * math.log2(math.e)

    def at_blk(b):
        return (cfg, b, mine)

    def at_uly(u):
        return (cfg, me, u)

    def partner(d):
        return lax.rem(mine + d, peers)

    barrier = pltpu.get_barrier_semaphore()
    for d in range(1, peers):
        pl.semaphore_signal(barrier, inc=1, device_id=at_uly(partner(d)), device_id_type=MESH)
    for b in (above, below, pair):
        pl.semaphore_signal(barrier, inc=1, device_id=at_blk(b), device_id_type=MESH)

    loads = [
        pltpu.make_async_copy(source, target, load_sem.at[i])
        for i, (source, target) in enumerate(((keys_hbm, keys), (values_hbm, values), (queries_hbm, queries)))
    ]
    for load in loads:
        load.start()

    own = REACH * block

    def columns(u, h):
        return pl.ds(pl.multiple_of((u * heads + h) * hd, hd), hd)

    def rows_of(start, u):
        return pl.ds(pl.multiple_of(start + u * tokens, tokens), tokens)

    def normed(states, gain, u, h):
        wide = states[:, columns(u, h)].astype(jnp.float32)
        factor = lax.rsqrt(jnp.mean(wide * wide, axis=-1, keepdims=True) + 1e-06)
        return (wide * factor * gain[...]).astype(jnp.bfloat16)

    def norm(kind, h):
        states, gain, target = (queries, query_gain, queries_out) if kind == 2 else (keys, key_gain, keys_out)

        def one(u, carry):
            target[h, u] = normed(states, gain, u, h)
            return carry

        lax.fori_loop(0, peers, one, 0)

    def spread(kind, h):
        n = units.index((h, kind)) if kind < 2 else None
        if kind == 2:
            landing = queries_in.at[h, rows_of(0, mine), :]
            queries_in[h, rows_of(0, mine), :] = queries_out[h, mine]
        elif kind == 1:
            landing = kv.at[h, 1, rows_of(own, mine), :]
            kv[h, 1, rows_of(own, mine), :] = values[:, columns(mine, h)]
        else:
            landing = kv.at[h, 0, rows_of(own, mine), :]
            kv[h, 0, rows_of(own, mine), :] = keys_out[h, mine]

        def send(d, carry):
            u = partner(d)
            if kind == 2:
                source = queries_out.at[h, u]
            elif kind == 1:
                source = values.at[:, columns(u, h)]
            else:
                source = keys_out.at[h, u]
            arrival = early_recv.at[n, d] if n is not None and n < EARLY else uly_recv.at[kind, h]
            pltpu.make_async_remote_copy(
                source, landing, uly_send.at[kind, h], arrival, device_id=at_uly(u), device_id_type=MESH,
            ).start()
            return carry

        lax.fori_loop(1, peers, send, 0)

    rest = (peers - 1) * tokens

    def wait_bytes(ref, sem):
        pltpu.make_async_copy(ref, ref, sem).wait()

    def wait_spread(kind, h):
        ref = queries_in.at[h, pl.ds(0, rest), :] if kind == 2 else kv.at[h, kind, pl.ds(own, rest), :]
        wait_bytes(ref, uly_recv.at[kind, h])

    sent = []

    def remote(unit, source, target, rows, send, recv, to):
        h, which = unit
        copy = pltpu.make_async_remote_copy(
            kv.at[h, which, pl.ds(source, rows), :], kv.at[h, which, pl.ds(target, rows), :],
            send, recv, device_id=at_blk(to), device_id_type=MESH,
        )
        copy.start()
        sent.append(copy)
        return copy

    def ring(unit, slot, source, target, rows, to):
        return remote(unit, source, target, rows, ring_send.at[(*unit, slot)], ring_recv.at[(*unit, slot)], to)

    def share(unit, slot, source):
        target = pl.multiple_of(source + (2 * core - 1) * block, block)
        return remote(unit, source, target, block, pair_send.at[(*unit, slot)], pair_recv.at[(*unit, slot)], pair)

    units = [(h, which) for h in range(heads) for which in (1, 0)]
    n_units = len(units)
    ringed, shared = {}, {}

    def own_in_pieces(k):
        h, which = unit = units[k]

        def forward(u):
            for slot, target, to in ((0, own - 2 * block, above), (1, own + 2 * block, below)):
                pltpu.make_async_remote_copy(
                    kv.at[h, which, rows_of(own, u), :], kv.at[h, which, rows_of(target, u), :],
                    ring_send.at[h, which, slot], ring_recv.at[h, which, slot],
                    device_id=at_blk(to), device_id_type=MESH,
                ).start()

        def one(d, carry):
            u = lax.rem(mine + peers - d, peers)
            wait_bytes(kv.at[h, which, rows_of(own, u), :], early_recv.at[k, d])
            forward(u)
            return carry

        forward(mine)
        lax.fori_loop(1, peers, one, 0)
        for slot, target, to in ((0, own - 2 * block, above), (1, own + 2 * block, below)):
            ringed[k, slot] = pltpu.make_async_remote_copy(
                kv.at[h, which, pl.ds(own, block), :], kv.at[h, which, pl.ds(target, block), :],
                ring_send.at[h, which, slot], ring_recv.at[h, which, slot],
                device_id=at_blk(to), device_id_type=MESH,
            )
            sent.append(ringed[k, slot])
        shared[k, 0] = share(unit, 0, own)

    far_source = own + (4 - 8 * core) * block
    far_target = own + (6 - 12 * core) * block
    far_to = lax.rem(me + blocks + 4 * core - 2, blocks)

    def piece_start(i):
        return (LOWER_FIRST[i] + core * (UPPER_FIRST[i] - LOWER_FIRST[i])) * TILE

    def step_own(k):
        if k < EARLY:
            own_in_pieces(k)
        elif k < n_units:
            unit = units[k]
            wait_spread(unit[1], unit[0])
            ringed[k, 0] = ring(unit, 0, own, own - 2 * block, block, above)
            ringed[k, 1] = ring(unit, 1, own, own + 2 * block, block, below)
            shared[k, 0] = share(unit, 0, own)

    def step_next(n):
        if not 0 <= n < n_units:
            return
        unit = units[n]
        ringed[n, 0].wait_recv()
        ringed[n, 2] = ring(unit, 2, own - 2 * block, own - 4 * block, block, above)
        ringed[n, 1].wait_recv()
        ringed[n, 3] = ring(unit, 3, own + 2 * block, own + 4 * block, block, below)
        shared[n, 1] = share(unit, 1, own - 2 * block)
        shared[n, 2] = share(unit, 2, own + 2 * block)

    def step_far(n):
        if not 0 <= n < n_units:
            return
        unit = units[n]
        ringed[n, 2].wait_recv()
        ringed[n, 3].wait_recv()
        ringed[n, 5] = ring(
            unit, 5,
            pl.multiple_of(own - 3 * block - TILE + core * (7 * block + TILE), TILE),
            pl.multiple_of(own - 5 * block - TILE + core * (11 * block + TILE), TILE),
            TILE, lax.rem(me + blocks + 2 - 4 * core, blocks),
        )
        if n == n_units - 1:
            for i, size in enumerate(PIECES):
                start = piece_start(i)
                ringed[n, 6 + i] = remote(
                    unit, pl.multiple_of(far_source + start, TILE), pl.multiple_of(far_target + start, TILE),
                    size * TILE, tail_send.at[i], tail_recv.at[i], far_to,
                )
        else:
            ringed[n, 4] = ring(
                unit, 4, pl.multiple_of(far_source, block), pl.multiple_of(far_target, block), block, far_to
            )
        shared[n, 3] = share(unit, 3, own - 4 * block)
        shared[n, 4] = share(unit, 4, own + 4 * block)

    def step_last(n):
        if not 0 <= n < n_units - 1:
            return
        ringed[n, 5].wait_recv()
        ringed[n, 4].wait_recv()
        shared[n, 5] = share(units[n], 5, pl.multiple_of(far_target, block))

    def share_piece(i):
        n = n_units - 1
        ringed[n, 6 + i].wait_recv()
        source = pl.multiple_of(far_target + piece_start(i), TILE)
        target = pl.multiple_of(far_target + piece_start(i) + (2 * core - 1) * block, TILE)
        shared[n, 6 + i] = remote(
            units[n], source, target, PIECES[i] * TILE, tail_pair_send.at[i], tail_pair_recv.at[i], pair
        )

    def build_mask():
        shape = (16, SPAN)
        row = lax.broadcasted_iota(jnp.int32, shape, 0)
        place = lax.broadcasted_iota(jnp.int32, shape, 1) // TILE
        centre = (row // 3 - 1) * FRAME + (row % 3 - 1) * WIDE

        def one(t, carry):
            tile = centre + place + (me * tiles + t - 1 - lax.rem(t, GROUP))
            live = jnp.zeros(shape, jnp.float32)
            count = counts[0, t]
            for n in range(neighbors.shape[1]):
                entry = jnp.where(n < count, neighbors[t, n], -(2 ** 20))
                live = jnp.where(tile == entry, 1.0, live)
            mask[t] = live
            return carry

        lax.fori_loop(0, tiles, one, 0)

    def attend(h, windows, first=False, last=False, begin=0, end=None):
        rows = GROUP * TILE

        def group(g, carry):
            t = g * GROUP
            mine_rows = pl.ds(pl.multiple_of(t * TILE, rows), rows)
            q = queries_in[h, mine_rows, :]
            if first:
                sums = jnp.zeros((rows, 128), jnp.float32)
                result = jnp.zeros((rows, hd), jnp.float32)
            else:
                sums = total[h, mine_rows, :]
                result = acc[h, mine_rows, :]

            def near(w):
                return pl.ds(pl.multiple_of(own + (t + CENTRES[w] - 1) * TILE, TILE), SPAN)

            def score(w):
                return lax.dot_general(
                    q, kv[h, 0, near(w), :], (((1,), (1,)), ((), ())), preferred_element_type=jnp.float32
                )

            scores = score(windows[0])
            for i, w in enumerate(windows):
                coming = score(windows[i + 1]) if i + 1 < len(windows) else None
                live = jnp.concatenate(
                    [jnp.broadcast_to(mask[t + a, pl.ds(w, 1), :], (TILE, SPAN)) for a in range(GROUP)], axis=0
                )
                weights = jnp.exp2(scores * scale) * live
                for part in range(0, SPAN, 128):
                    sums = sums + weights[:, part : part + 128]
                result = result + jnp.dot(
                    weights.astype(jnp.bfloat16), kv[h, 1, near(w), :], preferred_element_type=jnp.float32
                )
                scores = coming
            if last:
                mixed[h, mine_rows, :] = (result / jnp.sum(sums, axis=-1, keepdims=True)).astype(jnp.bfloat16)
            else:
                total[h, mine_rows, :] = sums
                acc[h, mine_rows, :] = result
            return carry

        lax.fori_loop(begin, tiles // GROUP if end is None else end, group, 0, unroll=2)

    def near_part(h):
        wait_spread(2, h)
        for which in (1, 0):
            n = units.index((h, which))
            for slot in (0, 1, 2):
                shared[n, slot].wait_recv()
        attend(h, NEAR, first=True)

    def middle_waits(h):
        for which in (1, 0):
            n = units.index((h, which))
            for slot in (3, 4):
                shared[n, slot].wait_recv()

    def middle_part(h):
        middle_waits(h)
        attend(h, MIDDLE)

    def send_back(h, u):
        source = mixed.at[h, rows_of(0, u), :]
        landing = out.at[:, columns(mine, h)]

        @pl.when(u != mine)
        def _():
            pltpu.make_async_remote_copy(
                source, landing, back_send.at[h], back_recv.at[h], device_id=at_uly(u), device_id_type=MESH,
            ).start()

        @pl.when(u == mine)
        def _():
            pltpu.make_async_copy(source, landing, own_sem.at[h]).start()

    def far_part(h):
        for which in (1, 0):
            shared[units.index((h, which)), 5].wait_recv()
        attend(h, FAR, last=True)

        def send(u, carry):
            send_back(h, u)
            return carry

        lax.fori_loop(0, peers, send, 0)

    loads[0].wait()
    norm(0, 0)
    loads[1].wait()
    pl.semaphore_wait(barrier, 3 + peers - 1)
    spread(1, 0)
    spread(0, 0)
    step_own(0)
    norm(0, 1)
    spread(1, 1)
    spread(0, 1)
    step_own(1)
    norm(0, 2)
    spread(1, 2)
    spread(0, 2)
    step_next(0)
    loads[2].wait()
    for h in range(heads):
        norm(2, h)
        spread(2, h)
    build_mask()
    last_head = heads - 1
    for k in range(2, n_units + 2):
        step_own(k)
        step_next(k - 1)
        step_far(k - 2)
        if k == n_units + 1:
            break
        step_last(k - 3)
        if k == 3:
            near_part(0)
        elif k == 4:
            middle_part(0)
        elif k == 5:
            far_part(0)
            near_part(1)
        elif k == 6:
            middle_part(1)
            near_part(2)
    n = n_units - 1
    far_part(last_head - 1)
    step_last(n_units - 2)
    middle_waits(last_head)
    half = tiles // GROUP // 2
    attend(last_head, MIDDLE, begin=0, end=half)
    ringed[n, 5].wait_recv()
    for i in (0, 1):
        share_piece(i)
    attend(last_head, MIDDLE, begin=half)
    for i in (2, 3, 4):
        share_piece(i)
    shared[units.index((last_head, 1)), 5].wait_recv()
    shared[n, 6].wait_recv()
    for i in range(1, len(PIECES)):
        shared[n, 6 + i].wait_recv()
        attend(last_head, FAR, last=True, begin=2 * i - 2, end=2 * i)
        for u in (2 * i - 2, 2 * i - 1):
            send_back(last_head, u)

    for copy in sent:
        copy.wait_send()
    for h in range(heads):
        for kind in range(3):
            wait_bytes(queries_in.at[h, pl.ds(0, rest), :], uly_send.at[kind, h])
        wait_bytes(queries_in.at[h, pl.ds(0, rest), :], back_send.at[h])
        wait_bytes(queries_in.at[h, pl.ds(0, tokens), :], own_sem.at[h])
    for h in range(heads):
        wait_bytes(queries_in.at[h, pl.ds(0, rest), :], back_recv.at[h])


def solution(mesh):
    blocks, peers = mesh.shape["blk"], mesh.shape["uly"]

    def per_device(queries, keys, values, query_gain, key_gain, neighbors, counts):
        tokens, width = queries.shape
        hd = query_gain.shape[0]
        heads = width // hd // peers
        block = tokens * peers
        tiles = block // TILE
        vmem = pl.BlockSpec(memory_space=pltpu.VMEM)
        smem = pl.BlockSpec(memory_space=pltpu.SMEM)
        dma = pltpu.SemaphoreType.DMA
        return pl.pallas_call(
            functools.partial(kernel, blocks, peers, heads),
            out_shape=jax.ShapeDtypeStruct((tokens, width), jnp.bfloat16),
            in_specs=[smem, smem] + [pl.BlockSpec(memory_space=pl.ANY)] * 3 + [vmem] * 2,
            out_specs=pl.BlockSpec(memory_space=pl.ANY),
            scratch_shapes=[
                pltpu.VMEM((tokens, width), jnp.bfloat16),
                pltpu.VMEM((tokens, width), jnp.bfloat16),
                pltpu.VMEM((tokens, width), jnp.bfloat16),
                pltpu.VMEM((heads, 2, (2 * REACH + 1) * block, hd), jnp.bfloat16),
                pltpu.VMEM((heads, block, hd), jnp.bfloat16),
                pltpu.VMEM((heads, peers, tokens, hd), jnp.bfloat16),
                pltpu.VMEM((heads, peers, tokens, hd), jnp.bfloat16),
                pltpu.VMEM((heads, block, 128), jnp.float32),
                pltpu.VMEM((heads, block, hd), jnp.float32),
                pltpu.VMEM((tiles, 16, SPAN), jnp.float32),
                pltpu.VMEM((heads, block, hd), jnp.bfloat16),
                dma((3,)), dma((3, heads)), dma((3, heads)), dma((EARLY, peers)),
                dma((heads, 2, 6)), dma((heads, 2, 6)),
                dma((heads, 2, 6)), dma((heads, 2, 6)),
                dma((len(PIECES),)), dma((len(PIECES),)), dma((len(PIECES),)), dma((len(PIECES),)),
                dma((heads,)), dma((heads,)), dma((heads,)),
            ],
            compiler_params=pltpu.CompilerParams(
                collective_id=0, has_side_effects=True, vmem_limit_bytes=56 * 2 ** 20
            ),
        )(neighbors, counts.reshape(1, -1), queries, keys, values, query_gain.reshape(1, -1), key_gain.reshape(1, -1))

    tokens = P(("cfg", "blk", "uly"), None)
    return jax.shard_map(
        per_device,
        mesh=mesh,
        in_specs=(tokens, tokens, tokens, P(), P(), P("blk", None), P("blk")),
        out_specs=tokens,
        check_vma=False,
    )
```

```python
import functools
import math

import jax
import jax.numpy as jnp
from jax import lax
from jax.experimental import pallas as pl
from jax.experimental.pallas import tpu as pltpu
from jax.sharding import PartitionSpec as P

MESH = pl.DeviceIdType.MESH
TILE = 64
WIDE = 20
FRAME = 60
REACH = 6
GROUP = 2
SPAN = (GROUP + 2) * TILE
CENTRES = tuple(FRAME * t + WIDE * h for t in (-1, 0, 1) for h in (-1, 0, 1))
NEAR = (3, 4, 5)
MIDDLE = (1, 2, 6, 7)
FAR = (0, 8)


PIECES = (1, 5, 4, 4, 2)
LOWER_FIRST = (0, 1, 6, 10, 14)
UPPER_FIRST = (15, 0, 5, 9, 13)


def kernel(
    blocks, peers, heads,
    neighbors, counts, queries_hbm, keys_hbm, values_hbm, query_gain, key_gain,
    out,
    queries, keys, values, kv, queries_in, keys_out, queries_out, total, acc, mask, mixed,
    load_sem, uly_send, uly_recv, piece_recv, ring_send, ring_recv, pair_send, pair_recv,
    tail_send, tail_recv, tail_pair_send, tail_pair_recv, back_send, back_recv, own_sem,
):
    tokens = queries.shape[0]
    hd = query_gain.shape[1]
    block = tokens * peers
    tiles = block // TILE
    cfg, me, mine = lax.axis_index("cfg"), lax.axis_index("blk"), lax.axis_index("uly")
    core = lax.rem(me, 2)
    above, below = lax.rem(me + 2, blocks), lax.rem(me + blocks - 2, blocks)
    pair = me + 1 - 2 * core
    scale = hd ** -0.5 * math.log2(math.e)

    def at_blk(b):
        return (cfg, b, mine)

    def at_uly(u):
        return (cfg, me, u)

    def partner(d):
        return lax.rem(mine + d, peers)

    barrier = pltpu.get_barrier_semaphore()
    for d in range(1, peers):
        pl.semaphore_signal(barrier, inc=1, device_id=at_uly(partner(d)), device_id_type=MESH)
    for b in (above, below, pair):
        pl.semaphore_signal(barrier, inc=1, device_id=at_blk(b), device_id_type=MESH)

    loads = [
        pltpu.make_async_copy(source, target, load_sem.at[i])
        for i, (source, target) in enumerate(((keys_hbm, keys), (values_hbm, values), (queries_hbm, queries)))
    ]
    for load in loads:
        load.start()

    own = REACH * block

    def columns(u, h):
        return pl.ds(pl.multiple_of((u * heads + h) * hd, hd), hd)

    def rows_of(start, u):
        return pl.ds(pl.multiple_of(start + u * tokens, tokens), tokens)

    def normed(states, gain, u, h):
        wide = states[:, columns(u, h)].astype(jnp.float32)
        factor = lax.rsqrt(jnp.mean(wide * wide, axis=-1, keepdims=True) + 1e-06)
        return (wide * factor * gain[...]).astype(jnp.bfloat16)

    def norm(kind, h):
        states, gain, target = (queries, query_gain, queries_out) if kind == 2 else (keys, key_gain, keys_out)

        def one(u, carry):
            target[h, u] = normed(states, gain, u, h)
            return carry

        lax.fori_loop(0, peers, one, 0)

    def spread(kind, h):
        if kind == 2:
            landing = queries_in.at[h, rows_of(0, mine), :]
            queries_in[h, rows_of(0, mine), :] = queries_out[h, mine]
        else:
            landing = kv.at[h, kind, rows_of(own, mine), :]

        def send(d, carry):
            u = partner(d)
            if kind == 2:
                source = queries_out.at[h, u]
            elif kind == 1:
                source = values.at[:, columns(u, h)]
            else:
                source = keys_out.at[h, u]
            arrival = uly_recv.at[h] if kind == 2 else piece_recv.at[h, kind, d]
            pltpu.make_async_remote_copy(
                source, landing, uly_send.at[kind, h], arrival, device_id=at_uly(u), device_id_type=MESH,
            ).start()
            return carry

        lax.fori_loop(1, peers, send, 0)

    rest = (peers - 1) * tokens

    def wait_bytes(ref, sem):
        pltpu.make_async_copy(ref, ref, sem).wait()

    sent = []

    def remote(unit, source, target, rows, send, recv, to):
        h, which = unit
        copy = pltpu.make_async_remote_copy(
            kv.at[h, which, pl.ds(source, rows), :], kv.at[h, which, pl.ds(target, rows), :],
            send, recv, device_id=at_blk(to), device_id_type=MESH,
        )
        copy.start()
        sent.append(copy)
        return copy

    def ring(unit, slot, source, target, rows, to):
        return remote(unit, source, target, rows, ring_send.at[(*unit, slot)], ring_recv.at[(*unit, slot)], to)

    def share(unit, slot, source):
        target = pl.multiple_of(source + (2 * core - 1) * block, block)
        return remote(unit, source, target, block, pair_send.at[(*unit, slot)], pair_recv.at[(*unit, slot)], pair)

    units = [(h, which) for h in range(heads) for which in (1, 0)]
    n_units = len(units)
    ringed, shared = {}, {}

    def forward(unit, u):
        h, which = unit
        for slot, target, to in ((0, own - 2 * block, above), (1, own + 2 * block, below)):
            pltpu.make_async_remote_copy(
                kv.at[h, which, rows_of(own, u), :], kv.at[h, which, rows_of(target, u), :],
                ring_send.at[h, which, slot], ring_recv.at[h, which, slot],
                device_id=at_blk(to), device_id_type=MESH,
            ).start()

    def store_own(unit):
        h, which = unit
        kv[h, which, rows_of(own, mine), :] = keys_out[h, mine] if which == 0 else values[:, columns(mine, h)]

    far_source = own + (4 - 8 * core) * block
    far_target = own + (6 - 12 * core) * block
    far_to = lax.rem(me + blocks + 4 * core - 2, blocks)

    def piece_start(i):
        return (LOWER_FIRST[i] + core * (UPPER_FIRST[i] - LOWER_FIRST[i])) * TILE

    def step_own(k):
        if k >= n_units:
            return
        h, which = unit = units[k]

        def one(d, carry):
            u = lax.rem(mine + peers - d, peers)
            wait_bytes(kv.at[h, which, rows_of(own, u), :], piece_recv.at[h, which, d])
            forward(unit, u)
            return carry

        lax.fori_loop(1, peers, one, 0)
        for slot, target, to in ((0, own - 2 * block, above), (1, own + 2 * block, below)):
            ringed[k, slot] = pltpu.make_async_remote_copy(
                kv.at[h, which, pl.ds(own, block), :], kv.at[h, which, pl.ds(target, block), :],
                ring_send.at[h, which, slot], ring_recv.at[h, which, slot],
                device_id=at_blk(to), device_id_type=MESH,
            )
            sent.append(ringed[k, slot])
        shared[k, 0] = share(unit, 0, own)

    def step_next(n):
        if not 0 <= n < n_units:
            return
        unit = units[n]
        ringed[n, 0].wait_recv()
        ringed[n, 2] = ring(unit, 2, own - 2 * block, own - 4 * block, block, above)
        ringed[n, 1].wait_recv()
        ringed[n, 3] = ring(unit, 3, own + 2 * block, own + 4 * block, block, below)
        shared[n, 1] = share(unit, 1, own - 2 * block)
        shared[n, 2] = share(unit, 2, own + 2 * block)

    def step_far(n):
        if not 0 <= n < n_units:
            return
        unit = units[n]
        ringed[n, 2].wait_recv()
        ringed[n, 3].wait_recv()
        ringed[n, 5] = ring(
            unit, 5,
            pl.multiple_of(own - 3 * block - TILE + core * (7 * block + TILE), TILE),
            pl.multiple_of(own - 5 * block - TILE + core * (11 * block + TILE), TILE),
            TILE, lax.rem(me + blocks + 2 - 4 * core, blocks),
        )
        if n == n_units - 1:
            for i, size in enumerate(PIECES):
                start = piece_start(i)
                ringed[n, 6 + i] = remote(
                    unit, pl.multiple_of(far_source + start, TILE), pl.multiple_of(far_target + start, TILE),
                    size * TILE, tail_send.at[i], tail_recv.at[i], far_to,
                )
        else:
            ringed[n, 4] = ring(
                unit, 4, pl.multiple_of(far_source, block), pl.multiple_of(far_target, block), block, far_to
            )
        shared[n, 3] = share(unit, 3, own - 4 * block)
        shared[n, 4] = share(unit, 4, own + 4 * block)

    def step_last(n):
        if not 0 <= n < n_units - 1:
            return
        ringed[n, 5].wait_recv()
        ringed[n, 4].wait_recv()
        shared[n, 5] = share(units[n], 5, pl.multiple_of(far_target, block))

    def share_piece(i):
        n = n_units - 1
        ringed[n, 6 + i].wait_recv()
        source = pl.multiple_of(far_target + piece_start(i), TILE)
        target = pl.multiple_of(far_target + piece_start(i) + (2 * core - 1) * block, TILE)
        shared[n, 6 + i] = remote(
            units[n], source, target, PIECES[i] * TILE, tail_pair_send.at[i], tail_pair_recv.at[i], pair
        )

    def build_mask():
        shape = (16, SPAN)
        row = lax.broadcasted_iota(jnp.int32, shape, 0)
        place = lax.broadcasted_iota(jnp.int32, shape, 1) // TILE
        centre = (row // 3 - 1) * FRAME + (row % 3 - 1) * WIDE

        def one(t, carry):
            tile = centre + place + (me * tiles + t - 1 - lax.rem(t, GROUP))
            live = jnp.zeros(shape, jnp.float32)
            count = counts[0, t]
            for n in range(neighbors.shape[1]):
                entry = jnp.where(n < count, neighbors[t, n], -(2 ** 20))
                live = jnp.where(tile == entry, 1.0, live)
            mask[t] = live
            return carry

        lax.fori_loop(0, tiles, one, 0)

    def attend(h, windows, first=False, last=False, begin=0, end=None):
        rows = GROUP * TILE

        def group(g, carry):
            t = g * GROUP
            mine_rows = pl.ds(pl.multiple_of(t * TILE, rows), rows)
            q = queries_in[h, mine_rows, :]
            if first:
                sums = jnp.zeros((rows, 128), jnp.float32)
                result = jnp.zeros((rows, hd), jnp.float32)
            else:
                sums = total[h, mine_rows, :]
                result = acc[h, mine_rows, :]

            def near(w):
                return pl.ds(pl.multiple_of(own + (t + CENTRES[w] - 1) * TILE, TILE), SPAN)

            def score(w):
                return lax.dot_general(
                    q, kv[h, 0, near(w), :], (((1,), (1,)), ((), ())), preferred_element_type=jnp.float32
                )

            scores = score(windows[0])
            for i, w in enumerate(windows):
                coming = score(windows[i + 1]) if i + 1 < len(windows) else None
                live = jnp.concatenate(
                    [jnp.broadcast_to(mask[t + a, pl.ds(w, 1), :], (TILE, SPAN)) for a in range(GROUP)], axis=0
                )
                weights = jnp.exp2(scores * scale) * live
                for part in range(0, SPAN, 128):
                    sums = sums + weights[:, part : part + 128]
                result = result + jnp.dot(
                    weights.astype(jnp.bfloat16), kv[h, 1, near(w), :], preferred_element_type=jnp.float32
                )
                scores = coming
            if last:
                mixed[h, mine_rows, :] = (result / jnp.sum(sums, axis=-1, keepdims=True)).astype(jnp.bfloat16)
            else:
                total[h, mine_rows, :] = sums
                acc[h, mine_rows, :] = result
            return carry

        lax.fori_loop(begin, tiles // GROUP if end is None else end, group, 0, unroll=2)

    def near_part(h):
        wait_bytes(queries_in.at[h, pl.ds(0, rest), :], uly_recv.at[h])
        for which in (1, 0):
            n = units.index((h, which))
            for slot in (0, 1, 2):
                shared[n, slot].wait_recv()
        attend(h, NEAR, first=True)

    def middle_waits(h):
        for which in (1, 0):
            n = units.index((h, which))
            for slot in (3, 4):
                shared[n, slot].wait_recv()

    def middle_part(h):
        middle_waits(h)
        attend(h, MIDDLE)

    def send_back(h, u):
        source = mixed.at[h, rows_of(0, u), :]
        landing = out.at[:, columns(mine, h)]

        @pl.when(u != mine)
        def _():
            pltpu.make_async_remote_copy(
                source, landing, back_send.at[h], back_recv.at[h], device_id=at_uly(u), device_id_type=MESH,
            ).start()

        @pl.when(u == mine)
        def _():
            pltpu.make_async_copy(source, landing, own_sem.at[h]).start()

    def far_part(h):
        for which in (1, 0):
            shared[units.index((h, which)), 5].wait_recv()
        attend(h, FAR, last=True)

        def send(u, carry):
            send_back(h, u)
            return carry

        lax.fori_loop(0, peers, send, 0)

    loads[0].wait()
    norm(0, 0)
    store_own((0, 0))
    loads[1].wait()
    store_own((0, 1))
    pl.semaphore_wait(barrier, 3 + peers - 1)
    forward((0, 1), mine)
    spread(1, 0)
    forward((0, 0), mine)
    spread(0, 0)
    for h in range(1, heads):
        store_own((h, 1))
        forward((h, 1), mine)
    step_own(0)
    norm(0, 1)
    store_own((1, 0))
    forward((1, 0), mine)
    spread(1, 1)
    spread(0, 1)
    step_own(1)
    for h in range(2, heads):
        norm(0, h)
        store_own((h, 0))
        forward((h, 0), mine)
        spread(1, h)
        spread(0, h)
    step_next(0)
    loads[2].wait()
    for h in range(heads):
        norm(2, h)
        spread(2, h)
    build_mask()
    last_head = heads - 1
    for k in range(2, n_units + 2):
        step_own(k)
        step_next(k - 1)
        step_far(k - 2)
        if k == n_units + 1:
            break
        step_last(k - 3)
        if k == 3:
            near_part(0)
        elif k == 4:
            middle_part(0)
        elif k == 5:
            far_part(0)
            near_part(1)
        elif k == 6:
            middle_part(1)
            near_part(2)
    n = n_units - 1
    far_part(last_head - 1)
    step_last(n_units - 2)
    middle_waits(last_head)
    half = tiles // GROUP // 2
    attend(last_head, MIDDLE, begin=0, end=half)
    ringed[n, 5].wait_recv()
    for i in (0, 1):
        share_piece(i)
    attend(last_head, MIDDLE, begin=half)
    for i in (2, 3, 4):
        share_piece(i)
    shared[units.index((last_head, 1)), 5].wait_recv()
    shared[n, 6].wait_recv()
    for i in range(1, len(PIECES)):
        shared[n, 6 + i].wait_recv()
        attend(last_head, FAR, last=True, begin=2 * i - 2, end=2 * i)
        for u in (2 * i - 2, 2 * i - 1):
            send_back(last_head, u)

    for copy in sent:
        copy.wait_send()
    for h in range(heads):
        for kind in range(3):
            wait_bytes(queries_in.at[h, pl.ds(0, rest), :], uly_send.at[kind, h])
        wait_bytes(queries_in.at[h, pl.ds(0, rest), :], back_send.at[h])
        wait_bytes(queries_in.at[h, pl.ds(0, tokens), :], own_sem.at[h])
    for h in range(heads):
        wait_bytes(queries_in.at[h, pl.ds(0, rest), :], back_recv.at[h])


def solution(mesh):
    blocks, peers = mesh.shape["blk"], mesh.shape["uly"]

    def per_device(queries, keys, values, query_gain, key_gain, neighbors, counts):
        tokens, width = queries.shape
        hd = query_gain.shape[0]
        heads = width // hd // peers
        block = tokens * peers
        tiles = block // TILE
        vmem = pl.BlockSpec(memory_space=pltpu.VMEM)
        smem = pl.BlockSpec(memory_space=pltpu.SMEM)
        dma = pltpu.SemaphoreType.DMA
        return pl.pallas_call(
            functools.partial(kernel, blocks, peers, heads),
            out_shape=jax.ShapeDtypeStruct((tokens, width), jnp.bfloat16),
            in_specs=[smem, smem] + [pl.BlockSpec(memory_space=pl.ANY)] * 3 + [vmem] * 2,
            out_specs=pl.BlockSpec(memory_space=pl.ANY),
            scratch_shapes=[
                pltpu.VMEM((tokens, width), jnp.bfloat16),
                pltpu.VMEM((tokens, width), jnp.bfloat16),
                pltpu.VMEM((tokens, width), jnp.bfloat16),
                pltpu.VMEM((heads, 2, (2 * REACH + 1) * block, hd), jnp.bfloat16),
                pltpu.VMEM((heads, block, hd), jnp.bfloat16),
                pltpu.VMEM((heads, peers, tokens, hd), jnp.bfloat16),
                pltpu.VMEM((heads, peers, tokens, hd), jnp.bfloat16),
                pltpu.VMEM((heads, block, 128), jnp.float32),
                pltpu.VMEM((heads, block, hd), jnp.float32),
                pltpu.VMEM((tiles, 16, SPAN), jnp.float32),
                pltpu.VMEM((heads, block, hd), jnp.bfloat16),
                dma((3,)), dma((3, heads)), dma((heads,)), dma((heads, 2, peers)),
                dma((heads, 2, 6)), dma((heads, 2, 6)),
                dma((heads, 2, 6)), dma((heads, 2, 6)),
                dma((len(PIECES),)), dma((len(PIECES),)), dma((len(PIECES),)), dma((len(PIECES),)),
                dma((heads,)), dma((heads,)), dma((heads,)),
            ],
            compiler_params=pltpu.CompilerParams(
                collective_id=0, has_side_effects=True, vmem_limit_bytes=56 * 2 ** 20
            ),
        )(neighbors, counts.reshape(1, -1), queries, keys, values, query_gain.reshape(1, -1), key_gain.reshape(1, -1))

    tokens = P(("cfg", "blk", "uly"), None)
    return jax.shard_map(
        per_device,
        mesh=mesh,
        in_specs=(tokens, tokens, tokens, P(), P(), P("blk", None), P("blk")),
        out_specs=tokens,
        check_vma=False,
    )
```

```python
import functools
import math

import jax
import jax.numpy as jnp
from jax import lax
from jax.experimental import pallas as pl
from jax.experimental.pallas import tpu as pltpu
from jax.sharding import PartitionSpec as P

MESH = pl.DeviceIdType.MESH
TILE = 64
WIDE = 20
FRAME = 60
REACH = 6
GROUP = 2
SPAN = (GROUP + 2) * TILE
NEAR = (-WIDE, 0, WIDE)
AHEAD = (FRAME - WIDE, FRAME, FRAME + WIDE)
PARTS = 4
ROWS = GROUP * TILE


def kernel(
    blocks, peers, heads,
    counts, neighbors, queries_hbm, keys_hbm, values_hbm, query_gain, key_gain,
    out,
    queries, keys, values, kv, queries_in, keys_out, queries_out, total, acc, mask, mixed,
    lists, guest_lists, guests, guest_mixed, guest_total, returned, returned_total,
    load_sem, uly_send, uly_recv, piece_recv, ring_send, ring_recv, pair_send, pair_recv,
    push_send, push_recv, list_sem, return_send, return_recv, total_send, total_recv, back_send, back_recv, own_sem,
):
    tokens = queries.shape[0]
    hd = query_gain.shape[1]
    block = tokens * peers
    tiles = block // TILE
    cfg, me, mine = lax.axis_index("cfg"), lax.axis_index("blk"), lax.axis_index("uly")
    core = lax.rem(me, 2)
    above, below = lax.rem(me + 2, blocks), lax.rem(me + blocks - 2, blocks)
    sibling = me + 1 - 2 * core
    upper = lax.rem(me // 2, 2)
    side = 2 * upper - 1
    partner_blk = me - 2 * side
    outer = lax.rem(me + blocks + 2 * side, blocks)
    gets_far = core + upper == 1
    scale = hd ** -0.5 * math.log2(math.e)
    own = REACH * block
    units = [(h, which) for h in range(heads) for which in (1, 0)]
    n_units = len(units)

    def slot_row(step):
        return pl.multiple_of(own + step * block, block)

    @pl.when(gets_far)
    def _():
        for h, which in units:
            kv[h, which, pl.ds(slot_row(6 * side), TILE), :] = jnp.zeros((TILE, hd), jnp.bfloat16)

    @pl.when(jnp.logical_not(gets_far))
    def _():
        for h, which in units:
            kv[h, which, pl.ds(slot_row(5 * side), block // 2), :] = jnp.zeros((block // 2, hd), jnp.bfloat16)

    def at_blk(b):
        return (cfg, b, mine)

    def at_uly(u):
        return (cfg, me, u)

    def partner(d):
        return lax.rem(mine + d, peers)

    barrier = pltpu.get_barrier_semaphore()
    for d in range(1, peers):
        pl.semaphore_signal(barrier, inc=1, device_id=at_uly(partner(d)), device_id_type=MESH)
    for b in (above, below, sibling):
        pl.semaphore_signal(barrier, inc=1, device_id=at_blk(b), device_id_type=MESH)

    loads = [
        pltpu.make_async_copy(source, target, load_sem.at[i])
        for i, (source, target) in enumerate(((keys_hbm, keys), (values_hbm, values), (queries_hbm, queries)))
    ]
    for load in loads:
        load.start()

    def columns(u, h):
        return pl.ds(pl.multiple_of((u * heads + h) * hd, hd), hd)

    def rows_of(start, u):
        return pl.ds(pl.multiple_of(start + u * tokens, tokens), tokens)

    def normed(states, gain, u, h):
        wide = states[:, columns(u, h)].astype(jnp.float32)
        factor = lax.rsqrt(jnp.mean(wide * wide, axis=-1, keepdims=True) + 1e-06)
        return (wide * factor * gain[...]).astype(jnp.bfloat16)

    def norm(kind, h):
        states, gain, target = (queries, query_gain, queries_out) if kind == 2 else (keys, key_gain, keys_out)

        def one(u, carry):
            target[h, u] = normed(states, gain, u, h)
            return carry

        lax.fori_loop(0, peers, one, 0)

    def spread(kind, h):
        if kind == 2:
            landing = queries_in.at[h, rows_of(0, mine), :]
            queries_in[h, rows_of(0, mine), :] = queries_out[h, mine]
        else:
            landing = kv.at[h, kind, rows_of(own, mine), :]

        def send(d, carry):
            u = partner(d)
            if kind == 2:
                source = queries_out.at[h, u]
            elif kind == 1:
                source = values.at[:, columns(u, h)]
            else:
                source = keys_out.at[h, u]
            arrival = uly_recv.at[h] if kind == 2 else piece_recv.at[h, kind, d]
            pltpu.make_async_remote_copy(
                source, landing, uly_send.at[kind, h], arrival, device_id=at_uly(u), device_id_type=MESH,
            ).start()
            return carry

        lax.fori_loop(1, peers, send, 0)

    rest = (peers - 1) * tokens

    def wait_bytes(ref, sem):
        pltpu.make_async_copy(ref, ref, sem).wait()

    sent = []

    def copy_to(source, target, send, recv, b):
        copy = pltpu.make_async_remote_copy(
            source, target, send, recv, device_id=at_blk(b), device_id_type=MESH
        )
        copy.start()
        sent.append(copy)
        return copy

    def block_of(unit, step):
        return kv.at[(*unit, pl.ds(slot_row(step), block), slice(None))]

    def ring(unit, slot, source, target, to):
        return copy_to(
            block_of(unit, source), block_of(unit, target), ring_send.at[(*unit, slot)], ring_recv.at[(*unit, slot)], to
        )

    def share(unit, slot, step):
        return copy_to(
            block_of(unit, step), block_of(unit, step + 2 * core - 1),
            pair_send.at[(*unit, slot)], pair_recv.at[(*unit, slot)], sibling,
        )

    def far_rows(unit, step, many):
        if many:
            return kv.at[(*unit, pl.ds(pl.multiple_of(slot_row(step) + block // 2, block // 2), block // 2), slice(None))]
        start = pl.multiple_of(slot_row(step) + (1 - core) * (block - TILE), TILE)
        return kv.at[(*unit, pl.ds(start, TILE), slice(None))]

    def far_copy(unit, slot, source, target, to, many):
        for flag, half in ((many, True), (jnp.logical_not(many), False)):

            @pl.when(flag)
            def _():
                pltpu.make_async_remote_copy(
                    far_rows(unit, source, half), far_rows(unit, target, half),
                    ring_send.at[(*unit, slot)], ring_recv.at[(*unit, slot)],
                    device_id=at_blk(to), device_id_type=MESH,
                ).start()

    def far_wait(unit, sem, many):
        for flag, rows in ((many, block // 2), (jnp.logical_not(many), TILE)):

            @pl.when(flag)
            def _():
                wait_bytes(kv.at[(*unit, pl.ds(own, rows), slice(None))], sem)

    ringed, shared = {}, {}

    def forward(unit, u):
        h, which = unit
        for slot, target, to in ((0, own - 2 * block, above), (1, own + 2 * block, below)):
            pltpu.make_async_remote_copy(
                kv.at[h, which, rows_of(own, u), :], kv.at[h, which, rows_of(target, u), :],
                ring_send.at[h, which, slot], ring_recv.at[h, which, slot],
                device_id=at_blk(to), device_id_type=MESH,
            ).start()

    def store_own(unit):
        h, which = unit
        kv[h, which, rows_of(own, mine), :] = keys_out[h, mine] if which == 0 else values[:, columns(mine, h)]

    def step_own(k):
        if k >= n_units:
            return
        h, which = unit = units[k]

        def one(d, carry):
            u = lax.rem(mine + peers - d, peers)
            wait_bytes(kv.at[h, which, rows_of(own, u), :], piece_recv.at[h, which, d])
            forward(unit, u)
            return carry

        lax.fori_loop(1, peers, one, 0)
        for slot, target, to in ((0, -2, above), (1, 2, below)):
            ringed[k, slot] = pltpu.make_async_remote_copy(
                block_of(unit, 0), block_of(unit, target), ring_send.at[h, which, slot], ring_recv.at[h, which, slot],
                device_id=at_blk(to), device_id_type=MESH,
            )
            sent.append(ringed[k, slot])
        shared[k, 0] = share(unit, 0, 0)

    def step_next(n):
        unit = units[n]
        ringed[n, 0].wait_recv()
        ringed[n, 1].wait_recv()
        ringed[n, 2] = ring(unit, 2, -2 * side, -4 * side, outer)
        far_copy(unit, 3, 2 * side, 4 * side, partner_blk, gets_far)
        shared[n, 1] = share(unit, 1, -2)
        shared[n, 2] = share(unit, 2, 2)

    def step_second(n):
        ringed[n, 2].wait_recv()
        shared[n, 3] = share(units[n], 3, 4 * side)

    def step_far(n):
        unit = units[n]
        far_wait(unit, ring_recv.at[(*unit, 3)], jnp.logical_not(gets_far))
        far_copy(unit, 4, -4 * side, -6 * side, outer, jnp.logical_not(gets_far))

    def far_share(n):
        unit = units[n]
        far_wait(unit, ring_recv.at[(*unit, 4)], gets_far)

        @pl.when(gets_far)
        def _():
            pltpu.make_async_remote_copy(
                far_rows(unit, 6 * side, True), far_rows(unit, 6 * side + 2 * core - 1, True),
                pair_send.at[(*unit, 4)], pair_recv.at[(*unit, 4)], device_id=at_blk(sibling), device_id_type=MESH,
            ).start()

    def far_share_wait(n):
        unit = units[n]

        @pl.when(jnp.logical_not(gets_far))
        def _():
            wait_bytes(far_rows(unit, 0, True), pair_recv.at[(*unit, 4)])

    def push(h):
        wait_bytes(queries_in.at[h, pl.ds(0, rest), :], uly_recv.at[h])
        pushed[h] = copy_to(queries_in.at[h], guests.at[h], push_send.at[h], push_recv.at[h], partner_blk)

    pushed = {}

    def list_tiles():
        shape = neighbors.shape
        row = lax.broadcasted_iota(jnp.int32, shape, 0)
        count = jnp.zeros(shape, jnp.int32)
        for t in range(tiles):
            count = jnp.where(row == t, counts[0, t], count)
        live = lax.broadcasted_iota(jnp.int32, shape, 1) < count
        lists[...] = jnp.full(lists.shape, -(2 ** 20), jnp.int32)
        lists[:, : shape[1]] = jnp.where(live, neighbors[...], -(2 ** 20))

    def build_mask(first, centres, entries, blk):
        shape = (tiles, SPAN)
        row = lax.broadcasted_iota(jnp.int32, shape, 0)
        place = lax.broadcasted_iota(jnp.int32, shape, 1) // TILE
        base = blk * tiles + row - 1 - lax.rem(row, GROUP) + place
        listed = entries[...]
        for i, centre in enumerate(centres):
            live = jnp.zeros(shape, jnp.float32)
            for n in range(neighbors.shape[1]):
                live = jnp.where(base + centre == listed[:, n : n + 1], 1.0, live)
            for t in range(tiles):
                mask[t, first + i : first + i + 1, :] = live[t : t + 1, :]

    def windows_sum(h, t, q, windows, sums, result):
        def near(centre):
            return pl.ds(pl.multiple_of(own + (t + centre - 1) * TILE, TILE), SPAN)

        def score(centre):
            return lax.dot_general(
                q, kv[h, 0, near(centre), :], (((1,), (1,)), ((), ())), preferred_element_type=jnp.float32
            )

        scores = score(windows[0][0])
        for i, (centre, line) in enumerate(windows):
            coming = score(windows[i + 1][0]) if i + 1 < len(windows) else None
            live = jnp.concatenate(
                [jnp.broadcast_to(mask[t + a, line : line + 1, :], (TILE, SPAN)) for a in range(GROUP)], axis=0
            )
            weights = jnp.exp2(scores * scale) * live
            for part in range(0, SPAN, 128):
                sums = sums + weights[:, part : part + 128]
            result = result + jnp.dot(
                weights.astype(jnp.bfloat16), kv[h, 1, near(centre), :], preferred_element_type=jnp.float32
            )
            scores = coming
        return sums, result

    def over_groups(work, begin=0, end=PARTS):
        each = tiles // GROUP // PARTS

        def part(i, carry):
            for s in range(each):
                t = (i * each + s) * GROUP
                work(i, s, t, pl.ds(pl.multiple_of(t * TILE, ROWS), ROWS))
            return carry

        lax.fori_loop(begin, end, part, 0)

    zeros = functools.partial(jnp.zeros, dtype=jnp.float32)

    def home(h):
        for which in (1, 0):
            for slot in (0, 1, 2):
                shared[units.index((h, which)), slot].wait_recv()

        def work(i, s, t, rows):
            windows = [(centre, line) for line, centre in enumerate(NEAR)]
            total[h, rows, :], acc[h, rows, :] = windows_sum(
                h, t, queries_in[h, rows, :], windows, zeros((ROWS, 128)), zeros((ROWS, hd))
            )

        over_groups(work)

    def diagonal():
        return lax.broadcasted_iota(jnp.int32, (ROWS, 128), 0) == lax.broadcasted_iota(jnp.int32, (ROWS, 128), 1)

    return_copies = {}

    def guest(h):
        for which in (1, 0):
            shared[units.index((h, which)), 3].wait_recv()
        pushed[h].wait_recv()

        def work(i, s, t, rows):
            windows = [(side * (ahead - 2 * tiles), 6 + j) for j, ahead in enumerate(AHEAD)]
            sums, result = windows_sum(h, t, guests[h, rows, :], windows, zeros((ROWS, 128)), zeros((ROWS, hd)))
            guest_mixed[h, rows, :] = result.astype(jnp.bfloat16)
            column = jnp.sum(sums, axis=-1, keepdims=True)
            guest_total[h, i, s : s + 1, :] = jnp.sum(jnp.where(diagonal(), column, 0.0), axis=0, keepdims=True)

        for i in range(PARTS):
            over_groups(work, i, i + 1)
            rows = pl.ds(i * (block // PARTS), block // PARTS)
            return_copies[h, i, 0] = copy_to(
                guest_mixed.at[h, rows, :], returned.at[h, rows, :], return_send.at[h, i], return_recv.at[h, i], partner_blk
            )
            return_copies[h, i, 1] = copy_to(
                guest_total.at[h, i], returned_total.at[h, i], total_send.at[h, i], total_recv.at[h, i], partner_blk
            )

    def middle(h):
        def work(i, s, t, rows):
            windows = [(side * ahead, 3 + j) for j, ahead in enumerate(AHEAD[:2])]
            total[h, rows, :], acc[h, rows, :] = windows_sum(
                h, t, queries_in[h, rows, :], windows, total[h, rows, :], acc[h, rows, :]
            )

        over_groups(work)

    def finish(h):
        for which in (1, 0):
            far_share_wait(units.index((h, which)))

        def work(i, s, t, rows):
            sums, result = windows_sum(
                h, t, queries_in[h, rows, :], [(side * AHEAD[2], 5)], total[h, rows, :], acc[h, rows, :]
            )
            line = returned_total[h, i, s : s + 1, :]
            sums = sums + jnp.where(diagonal(), jnp.broadcast_to(line, (ROWS, 128)), 0.0)
            result = result + returned[h, rows, :].astype(jnp.float32)
            mixed[h, rows, :] = (result / jnp.sum(sums, axis=-1, keepdims=True)).astype(jnp.bfloat16)

        each = peers // PARTS
        for i in range(PARTS):
            return_copies[h, i, 0].wait_recv()
            return_copies[h, i, 1].wait_recv()
            over_groups(work, i, i + 1)
            for u in range(i * each, (i + 1) * each):
                send_back(h, u)

    def send_back(h, u):
        source = mixed.at[h, rows_of(0, u), :]
        landing = out.at[:, columns(mine, h)]

        @pl.when(u != mine)
        def _():
            pltpu.make_async_remote_copy(
                source, landing, back_send.at[h], back_recv.at[h], device_id=at_uly(u), device_id_type=MESH,
            ).start()

        @pl.when(u == mine)
        def _():
            pltpu.make_async_copy(source, landing, own_sem.at[h]).start()

    loads[0].wait()
    norm(0, 0)
    store_own((0, 0))
    loads[1].wait()
    store_own((0, 1))
    pl.semaphore_wait(barrier, 3 + peers - 1)
    forward((0, 1), mine)
    spread(1, 0)
    forward((0, 0), mine)
    spread(0, 0)
    for h in range(1, heads):
        store_own((h, 1))
        forward((h, 1), mine)
    step_own(0)
    norm(0, 1)
    store_own((1, 0))
    forward((1, 0), mine)
    spread(1, 1)
    spread(0, 1)
    step_own(1)
    loads[2].wait()
    norm(2, 0)
    spread(2, 0)
    for h in range(2, heads):
        norm(0, h)
        store_own((h, 0))
        forward((h, 0), mine)
        spread(1, h)
        spread(0, h)
    step_next(0)
    for h in range(1, heads):
        norm(2, h)
        spread(2, h)
    list_tiles()
    lists_copy = copy_to(lists, guest_lists, list_sem.at[0], list_sem.at[1], partner_blk)
    guest_total[...] = jnp.zeros(guest_total.shape, jnp.float32)
    step_own(2)
    push(0)
    step_next(1)
    step_second(0)
    build_mask(0, NEAR, lists, me)
    step_own(3)
    step_next(2)
    step_second(1)
    push(1)
    home(0)
    build_mask(3, [side * ahead for ahead in AHEAD], lists, me)
    lists_copy.wait_recv()
    build_mask(6, [side * ahead for ahead in AHEAD], guest_lists, partner_blk)
    step_own(4)
    step_next(3)
    step_second(2)
    push(2)
    guest(0)
    middle(0)
    step_own(5)
    step_next(4)
    step_second(3)
    home(1)
    step_next(5)
    for n in range(n_units - 1):
        step_far(n)
    step_second(4)
    guest(1)
    middle(1)
    home(2)
    step_far(n_units - 1)
    step_second(5)
    guest(2)
    for h in range(heads):
        far_share(2 * h)
        far_share(2 * h + 1)
        if h == heads - 1:
            middle(h)
        finish(h)

    for copy in sent:
        copy.wait_send()
    for unit in units:
        far_wait(unit, ring_send.at[(*unit, 3)], gets_far)
        far_wait(unit, ring_send.at[(*unit, 4)], jnp.logical_not(gets_far))

        @pl.when(gets_far)
        def _():
            wait_bytes(far_rows(unit, 0, True), pair_send.at[(*unit, 4)])

    for h in range(heads):
        for kind in range(3):
            wait_bytes(queries_in.at[h, pl.ds(0, rest), :], uly_send.at[kind, h])
        wait_bytes(queries_in.at[h, pl.ds(0, rest), :], back_send.at[h])
        wait_bytes(queries_in.at[h, pl.ds(0, tokens), :], own_sem.at[h])
    for h in range(heads):
        wait_bytes(queries_in.at[h, pl.ds(0, rest), :], back_recv.at[h])


def solution(mesh):
    blocks, peers = mesh.shape["blk"], mesh.shape["uly"]

    def per_device(queries, keys, values, query_gain, key_gain, neighbors, counts):
        tokens, width = queries.shape
        hd = query_gain.shape[0]
        heads = width // hd // peers
        block = tokens * peers
        tiles = block // TILE
        vmem = pl.BlockSpec(memory_space=pltpu.VMEM)
        smem = pl.BlockSpec(memory_space=pltpu.SMEM)
        dma = pltpu.SemaphoreType.DMA
        return pl.pallas_call(
            functools.partial(kernel, blocks, peers, heads),
            out_shape=jax.ShapeDtypeStruct((tokens, width), jnp.bfloat16),
            in_specs=[smem, vmem] + [pl.BlockSpec(memory_space=pl.ANY)] * 3 + [vmem] * 2,
            out_specs=pl.BlockSpec(memory_space=pl.ANY),
            scratch_shapes=[
                pltpu.VMEM((tokens, width), jnp.bfloat16),
                pltpu.VMEM((tokens, width), jnp.bfloat16),
                pltpu.VMEM((tokens, width), jnp.bfloat16),
                pltpu.VMEM((heads, 2, (2 * REACH + 1) * block, hd), jnp.bfloat16),
                pltpu.VMEM((heads, block, hd), jnp.bfloat16),
                pltpu.VMEM((heads, peers, tokens, hd), jnp.bfloat16),
                pltpu.VMEM((heads, peers, tokens, hd), jnp.bfloat16),
                pltpu.VMEM((heads, block, 128), jnp.float32),
                pltpu.VMEM((heads, block, hd), jnp.float32),
                pltpu.VMEM((tiles, 16, SPAN), jnp.float32),
                pltpu.VMEM((heads, block, hd), jnp.bfloat16),
                pltpu.VMEM((tiles, 128), jnp.int32),
                pltpu.VMEM((tiles, 128), jnp.int32),
                pltpu.VMEM((heads, block, hd), jnp.bfloat16),
                pltpu.VMEM((heads, block, hd), jnp.bfloat16),
                pltpu.VMEM((heads, PARTS, 8, 128), jnp.float32),
                pltpu.VMEM((heads, block, hd), jnp.bfloat16),
                pltpu.VMEM((heads, PARTS, 8, 128), jnp.float32),
                dma((3,)), dma((3, heads)), dma((heads,)), dma((heads, 2, peers)),
                dma((heads, 2, 5)), dma((heads, 2, 5)),
                dma((heads, 2, 5)), dma((heads, 2, 5)),
                dma((heads,)), dma((heads,)), dma((2,)),
                dma((heads, PARTS)), dma((heads, PARTS)), dma((heads, PARTS)), dma((heads, PARTS)),
                dma((heads,)), dma((heads,)), dma((heads,)),
            ],
            compiler_params=pltpu.CompilerParams(
                collective_id=0, has_side_effects=True, vmem_limit_bytes=56 * 2 ** 20
            ),
        )(counts.reshape(1, -1), neighbors, queries, keys, values, query_gain.reshape(1, -1), key_gain.reshape(1, -1))

    tokens = P(("cfg", "blk", "uly"), None)
    return jax.shard_map(
        per_device,
        mesh=mesh,
        in_specs=(tokens, tokens, tokens, P(), P(), P("blk", None), P("blk")),
        out_specs=tokens,
        check_vma=False,
    )
```

```python
import functools
import math

import jax
import jax.numpy as jnp
from jax import lax
from jax.experimental import pallas as pl
from jax.experimental.pallas import tpu as pltpu
from jax.sharding import PartitionSpec as P

MESH = pl.DeviceIdType.MESH
TILE = 64
WIDE = 20
FRAME = 60
REACH = 6
GROUP = 2
SPAN = (GROUP + 2) * TILE
NEAR = (-WIDE, 0, WIDE)
AHEAD = (FRAME - WIDE, FRAME, FRAME + WIDE)
PARTS = 4
ROWS = GROUP * TILE


def kernel(
    blocks, peers, heads,
    counts, neighbors, queries_hbm, keys_hbm, values_hbm, query_gain, key_gain,
    out,
    queries, keys, values, kv, queries_in, keys_out, queries_out, total, acc, mask, mixed,
    lists, guest_lists, guests, guest_mixed, guest_total, returned, returned_total,
    load_sem, uly_send, uly_recv, piece_recv, ring_send, ring_recv, pair_send, pair_recv,
    push_send, push_recv, list_sem, return_send, return_recv, total_send, total_recv, back_send, back_recv, own_sem,
):
    tokens = queries.shape[0]
    hd = query_gain.shape[1]
    block = tokens * peers
    tiles = block // TILE
    cfg, me, mine = lax.axis_index("cfg"), lax.axis_index("blk"), lax.axis_index("uly")
    core = lax.rem(me, 2)
    above, below = lax.rem(me + 2, blocks), lax.rem(me + blocks - 2, blocks)
    sibling = me + 1 - 2 * core
    upper = lax.rem(me // 2, 2)
    side = 2 * upper - 1
    partner_blk = me - 2 * side
    outer = lax.rem(me + blocks + 2 * side, blocks)
    outer_sibling = outer + 1 - 2 * core
    gets_half = core == upper
    gives_half = core + upper == 1
    gives_one = core + upper == 2
    gets_one = core - upper == 1
    is_one = core == 1
    scale = hd ** -0.5 * math.log2(math.e)
    own = REACH * block
    units = [(h, which) for h in range(heads) for which in (1, 0)]
    n_units = len(units)

    def slot_row(step):
        return pl.multiple_of(own + step * block, block)

    def at_blk(b):
        return (cfg, b, mine)

    def at_uly(u):
        return (cfg, me, u)

    def partner(d):
        return lax.rem(mine + d, peers)

    barrier = pltpu.get_barrier_semaphore()
    for d in range(1, peers):
        pl.semaphore_signal(barrier, inc=1, device_id=at_uly(partner(d)), device_id_type=MESH)
    for b in (above, below, sibling, outer_sibling):
        pl.semaphore_signal(barrier, inc=1, device_id=at_blk(b), device_id_type=MESH)

    loads = [
        pltpu.make_async_copy(source, target, load_sem.at[i])
        for i, (source, target) in enumerate(((keys_hbm, keys), (values_hbm, values), (queries_hbm, queries)))
    ]
    for load in loads:
        load.start()

    @pl.when(core == 0)
    def _():
        start = pl.multiple_of(own - 5 * block - TILE + upper * (11 * block + TILE), TILE)
        for h, which in units:
            kv[h, which, pl.ds(start, TILE), :] = jnp.zeros((TILE, hd), jnp.bfloat16)

    @pl.when(gets_half)
    def _():
        for h, which in units:
            kv[h, which, pl.ds(slot_row(5 * side), block // 2), :] = jnp.zeros((block // 2, hd), jnp.bfloat16)

    def columns(u, h):
        return pl.ds(pl.multiple_of((u * heads + h) * hd, hd), hd)

    def rows_of(start, u):
        return pl.ds(pl.multiple_of(start + u * tokens, tokens), tokens)

    def normed(states, gain, u, h):
        wide = states[:, columns(u, h)].astype(jnp.float32)
        factor = lax.rsqrt(jnp.mean(wide * wide, axis=-1, keepdims=True) + 1e-06)
        return (wide * factor * gain[...]).astype(jnp.bfloat16)

    def norm(kind, h):
        states, gain, target = (queries, query_gain, queries_out) if kind == 2 else (keys, key_gain, keys_out)

        def one(u, carry):
            target[h, u] = normed(states, gain, u, h)
            return carry

        lax.fori_loop(0, peers, one, 0)

    def spread(kind, h):
        if kind == 2:
            landing = queries_in.at[h, rows_of(0, mine), :]
            queries_in[h, rows_of(0, mine), :] = queries_out[h, mine]
        else:
            landing = kv.at[h, kind, rows_of(own, mine), :]

        def send(d, carry):
            u = partner(d)
            if kind == 2:
                source = queries_out.at[h, u]
            elif kind == 1:
                source = values.at[:, columns(u, h)]
            else:
                source = keys_out.at[h, u]
            arrival = uly_recv.at[h] if kind == 2 else piece_recv.at[h, kind, d]
            pltpu.make_async_remote_copy(
                source, landing, uly_send.at[kind, h], arrival, device_id=at_uly(u), device_id_type=MESH,
            ).start()
            return carry

        lax.fori_loop(1, peers, send, 0)

    rest = (peers - 1) * tokens

    def wait_bytes(ref, sem):
        pltpu.make_async_copy(ref, ref, sem).wait()

    sent = []

    def copy_to(source, target, send, recv, b):
        copy = pltpu.make_async_remote_copy(
            source, target, send, recv, device_id=at_blk(b), device_id_type=MESH
        )
        copy.start()
        sent.append(copy)
        return copy

    def block_of(unit, step):
        return kv.at[(*unit, pl.ds(slot_row(step), block), slice(None))]

    def ring(unit, slot, source, target, to):
        return copy_to(
            block_of(unit, source), block_of(unit, target), ring_send.at[(*unit, slot)], ring_recv.at[(*unit, slot)], to
        )

    def share(unit, slot, step):
        return copy_to(
            block_of(unit, step), block_of(unit, step + 2 * core - 1),
            pair_send.at[(*unit, slot)], pair_recv.at[(*unit, slot)], sibling,
        )

    def half_of(unit, step):
        return kv.at[(*unit, pl.ds(pl.multiple_of(slot_row(step) + block // 2, block // 2), block // 2), slice(None))]

    def tile_of(unit, step, tile):
        return kv.at[(*unit, pl.ds(pl.multiple_of(slot_row(step) + tile * TILE, TILE), TILE), slice(None))]

    def copy_if(flag, unit, slot, source, target, to):
        @pl.when(flag)
        def _():
            pltpu.make_async_remote_copy(
                source, target, ring_send.at[(*unit, slot)], ring_recv.at[(*unit, slot)],
                device_id=at_blk(to), device_id_type=MESH,
            ).start()

    def wait_if(flag, sem, rows):
        @pl.when(flag)
        def _():
            wait_bytes(kv.at[0, 0, pl.ds(own, rows), :], sem)

    ringed, shared = {}, {}

    def forward(unit, u):
        h, which = unit
        for slot, target, to in ((0, own - 2 * block, above), (1, own + 2 * block, below)):
            pltpu.make_async_remote_copy(
                kv.at[h, which, rows_of(own, u), :], kv.at[h, which, rows_of(target, u), :],
                ring_send.at[h, which, slot], ring_recv.at[h, which, slot],
                device_id=at_blk(to), device_id_type=MESH,
            ).start()

    def store_own(unit):
        h, which = unit
        kv[h, which, rows_of(own, mine), :] = keys_out[h, mine] if which == 0 else values[:, columns(mine, h)]

    def step_own(k):
        if k >= n_units:
            return
        h, which = unit = units[k]

        def one(d, carry):
            u = lax.rem(mine + peers - d, peers)
            wait_bytes(kv.at[h, which, rows_of(own, u), :], piece_recv.at[h, which, d])
            forward(unit, u)
            return carry

        lax.fori_loop(1, peers, one, 0)
        for slot, target, to in ((0, -2, above), (1, 2, below)):
            ringed[k, slot] = pltpu.make_async_remote_copy(
                block_of(unit, 0), block_of(unit, target), ring_send.at[h, which, slot], ring_recv.at[h, which, slot],
                device_id=at_blk(to), device_id_type=MESH,
            )
            sent.append(ringed[k, slot])
        shared[k, 0] = share(unit, 0, 0)

    def step_next(n):
        unit = units[n]
        ringed[n, 0].wait_recv()
        ringed[n, 1].wait_recv()
        ringed[n, 2] = ring(unit, 2, -2 * side, -4 * side, outer)
        copy_if(gives_half, unit, 3, half_of(unit, 2 * side), half_of(unit, 4 * side), partner_blk)
        copy_if(gives_one, unit, 3, tile_of(unit, 2, 0), tile_of(unit, 4, 0), partner_blk)
        shared[n, 1] = share(unit, 1, -2)
        shared[n, 2] = share(unit, 2, 2)

    def step_second(n):
        ringed[n, 2].wait_recv()
        shared[n, 3] = share(units[n], 3, 4 * side)

    def step_far(n):
        unit = units[n]
        last_tile = upper * (tiles - 1)
        wait_if(gets_half, ring_recv.at[(*unit, 3)], block // 2)
        wait_if(gets_one, ring_recv.at[(*unit, 3)], TILE)
        copy_if(
            gets_half, unit, 4, half_of(unit, -4 * side), half_of(unit, 2 * core - 1 - 6 * side), outer_sibling
        )
        copy_if(is_one, unit, 5, tile_of(unit, -4 * side, last_tile), tile_of(unit, -6 * side, last_tile), outer)

    def push(h):
        wait_bytes(queries_in.at[h, pl.ds(0, rest), :], uly_recv.at[h])
        pushed[h] = copy_to(queries_in.at[h], guests.at[h], push_send.at[h], push_recv.at[h], partner_blk)

    pushed = {}

    def list_tiles():
        shape = neighbors.shape
        row = lax.broadcasted_iota(jnp.int32, shape, 0)
        count = jnp.zeros(shape, jnp.int32)
        for t in range(tiles):
            count = jnp.where(row == t, counts[0, t], count)
        live = lax.broadcasted_iota(jnp.int32, shape, 1) < count
        lists[...] = jnp.full(lists.shape, -(2 ** 20), jnp.int32)
        lists[:, : shape[1]] = jnp.where(live, neighbors[...], -(2 ** 20))

    def build_mask(first, centres, entries, blk):
        shape = (tiles, SPAN)
        row = lax.broadcasted_iota(jnp.int32, shape, 0)
        place = lax.broadcasted_iota(jnp.int32, shape, 1) // TILE
        base = blk * tiles + row - 1 - lax.rem(row, GROUP) + place
        listed = entries[...]
        for i, centre in enumerate(centres):
            live = jnp.zeros(shape, jnp.float32)
            for n in range(neighbors.shape[1]):
                live = jnp.where(base + centre == listed[:, n : n + 1], 1.0, live)
            for t in range(tiles):
                mask[t, first + i : first + i + 1, :] = live[t : t + 1, :]

    def windows_sum(h, t, q, windows, sums, result):
        def near(centre):
            return pl.ds(pl.multiple_of(own + (t + centre - 1) * TILE, TILE), SPAN)

        def score(centre):
            return lax.dot_general(
                q, kv[h, 0, near(centre), :], (((1,), (1,)), ((), ())), preferred_element_type=jnp.float32
            )

        scores = score(windows[0][0])
        for i, (centre, line) in enumerate(windows):
            coming = score(windows[i + 1][0]) if i + 1 < len(windows) else None
            live = jnp.concatenate(
                [jnp.broadcast_to(mask[t + a, line : line + 1, :], (TILE, SPAN)) for a in range(GROUP)], axis=0
            )
            weights = jnp.exp2(scores * scale) * live
            for part in range(0, SPAN, 128):
                sums = sums + weights[:, part : part + 128]
            result = result + jnp.dot(
                weights.astype(jnp.bfloat16), kv[h, 1, near(centre), :], preferred_element_type=jnp.float32
            )
            scores = coming
        return sums, result

    def over_groups(work, begin=0, end=PARTS):
        each = tiles // GROUP // PARTS

        def part(i, carry):
            for s in range(each):
                t = (i * each + s) * GROUP
                work(i, s, t, pl.ds(pl.multiple_of(t * TILE, ROWS), ROWS))
            return carry

        lax.fori_loop(begin, end, part, 0)

    zeros = functools.partial(jnp.zeros, dtype=jnp.float32)

    def home(h):
        for which in (1, 0):
            for slot in (0, 1, 2):
                shared[units.index((h, which)), slot].wait_recv()

        def work(i, s, t, rows):
            windows = [(centre, line) for line, centre in enumerate(NEAR)]
            total[h, rows, :], acc[h, rows, :] = windows_sum(
                h, t, queries_in[h, rows, :], windows, zeros((ROWS, 128)), zeros((ROWS, hd))
            )

        over_groups(work)

    def diagonal():
        return lax.broadcasted_iota(jnp.int32, (ROWS, 128), 0) == lax.broadcasted_iota(jnp.int32, (ROWS, 128), 1)

    return_copies = {}

    def guest(h):
        for which in (1, 0):
            shared[units.index((h, which)), 3].wait_recv()
        pushed[h].wait_recv()

        def work(i, s, t, rows):
            windows = [(side * (ahead - 2 * tiles), 6 + j) for j, ahead in enumerate(AHEAD)]
            sums, result = windows_sum(h, t, guests[h, rows, :], windows, zeros((ROWS, 128)), zeros((ROWS, hd)))
            guest_mixed[h, rows, :] = result.astype(jnp.bfloat16)
            column = jnp.sum(sums, axis=-1, keepdims=True)
            guest_total[h, i, s : s + 1, :] = jnp.sum(jnp.where(diagonal(), column, 0.0), axis=0, keepdims=True)

        for i in range(PARTS):
            over_groups(work, i, i + 1)
            rows = pl.ds(i * (block // PARTS), block // PARTS)
            return_copies[h, i, 0] = copy_to(
                guest_mixed.at[h, rows, :], returned.at[h, rows, :], return_send.at[h, i], return_recv.at[h, i], partner_blk
            )
            return_copies[h, i, 1] = copy_to(
                guest_total.at[h, i], returned_total.at[h, i], total_send.at[h, i], total_recv.at[h, i], partner_blk
            )

    def middle(h):
        def work(i, s, t, rows):
            windows = [(side * ahead, 3 + j) for j, ahead in enumerate(AHEAD[:2])]
            total[h, rows, :], acc[h, rows, :] = windows_sum(
                h, t, queries_in[h, rows, :], windows, total[h, rows, :], acc[h, rows, :]
            )

        over_groups(work)

    def finish(h):
        for which in (1, 0):
            wait_if(gets_half, ring_recv.at[h, which, 4], block // 2)
            wait_if(is_one, ring_recv.at[h, which, 5], TILE)

        def work(i, s, t, rows):
            sums, result = windows_sum(
                h, t, queries_in[h, rows, :], [(side * AHEAD[2], 5)], total[h, rows, :], acc[h, rows, :]
            )
            line = returned_total[h, i, s : s + 1, :]
            sums = sums + jnp.where(diagonal(), jnp.broadcast_to(line, (ROWS, 128)), 0.0)
            result = result + returned[h, rows, :].astype(jnp.float32)
            mixed[h, rows, :] = (result / jnp.sum(sums, axis=-1, keepdims=True)).astype(jnp.bfloat16)

        each = peers // PARTS
        for i in range(PARTS):
            return_copies[h, i, 0].wait_recv()
            return_copies[h, i, 1].wait_recv()
            over_groups(work, i, i + 1)
            for u in range(i * each, (i + 1) * each):
                send_back(h, u)

    def send_back(h, u):
        source = mixed.at[h, rows_of(0, u), :]
        landing = out.at[:, columns(mine, h)]

        @pl.when(u != mine)
        def _():
            pltpu.make_async_remote_copy(
                source, landing, back_send.at[h], back_recv.at[h], device_id=at_uly(u), device_id_type=MESH,
            ).start()

        @pl.when(u == mine)
        def _():
            pltpu.make_async_copy(source, landing, own_sem.at[h]).start()

    loads[0].wait()
    norm(0, 0)
    store_own((0, 0))
    loads[1].wait()
    store_own((0, 1))
    pl.semaphore_wait(barrier, 4 + peers - 1)
    forward((0, 1), mine)
    spread(1, 0)
    forward((0, 0), mine)
    spread(0, 0)
    for h in range(1, heads):
        store_own((h, 1))
        forward((h, 1), mine)
    step_own(0)
    norm(0, 1)
    store_own((1, 0))
    forward((1, 0), mine)
    spread(1, 1)
    spread(0, 1)
    step_own(1)
    loads[2].wait()
    norm(2, 0)
    spread(2, 0)
    for h in range(2, heads):
        norm(0, h)
        store_own((h, 0))
        forward((h, 0), mine)
        spread(1, h)
        spread(0, h)
    step_next(0)
    for h in range(1, heads):
        norm(2, h)
        spread(2, h)
    list_tiles()
    lists_copy = copy_to(lists, guest_lists, list_sem.at[0], list_sem.at[1], partner_blk)
    guest_total[...] = jnp.zeros(guest_total.shape, jnp.float32)
    step_own(2)
    push(0)
    step_next(1)
    step_second(0)
    build_mask(0, NEAR, lists, me)
    step_own(3)
    step_next(2)
    step_second(1)
    push(1)
    home(0)
    build_mask(3, [side * ahead for ahead in AHEAD], lists, me)
    lists_copy.wait_recv()
    build_mask(6, [side * ahead for ahead in AHEAD], guest_lists, partner_blk)
    step_own(4)
    step_next(3)
    step_second(2)
    push(2)
    guest(0)
    middle(0)
    step_own(5)
    step_next(4)
    step_far(0)
    step_far(1)
    step_second(3)
    home(1)
    step_next(5)
    step_far(2)
    step_far(3)
    step_far(4)
    guest(1)
    step_second(4)
    middle(1)
    finish(0)
    home(2)
    step_far(5)
    step_second(5)
    guest(2)
    finish(1)
    middle(2)
    finish(2)

    for copy in sent:
        copy.wait_send()
    for unit in units:
        wait_if(gives_half, ring_send.at[(*unit, 3)], block // 2)
        wait_if(gives_one, ring_send.at[(*unit, 3)], TILE)
        wait_if(gets_half, ring_send.at[(*unit, 4)], block // 2)
        wait_if(is_one, ring_send.at[(*unit, 5)], TILE)
    for h in range(heads):
        for kind in range(3):
            wait_bytes(queries_in.at[h, pl.ds(0, rest), :], uly_send.at[kind, h])
        wait_bytes(queries_in.at[h, pl.ds(0, rest), :], back_send.at[h])
        wait_bytes(queries_in.at[h, pl.ds(0, tokens), :], own_sem.at[h])
    for h in range(heads):
        wait_bytes(queries_in.at[h, pl.ds(0, rest), :], back_recv.at[h])


def solution(mesh):
    blocks, peers = mesh.shape["blk"], mesh.shape["uly"]

    def per_device(queries, keys, values, query_gain, key_gain, neighbors, counts):
        tokens, width = queries.shape
        hd = query_gain.shape[0]
        heads = width // hd // peers
        block = tokens * peers
        tiles = block // TILE
        vmem = pl.BlockSpec(memory_space=pltpu.VMEM)
        smem = pl.BlockSpec(memory_space=pltpu.SMEM)
        dma = pltpu.SemaphoreType.DMA
        return pl.pallas_call(
            functools.partial(kernel, blocks, peers, heads),
            out_shape=jax.ShapeDtypeStruct((tokens, width), jnp.bfloat16),
            in_specs=[smem, vmem] + [pl.BlockSpec(memory_space=pl.ANY)] * 3 + [vmem] * 2,
            out_specs=pl.BlockSpec(memory_space=pl.ANY),
            scratch_shapes=[
                pltpu.VMEM((tokens, width), jnp.bfloat16),
                pltpu.VMEM((tokens, width), jnp.bfloat16),
                pltpu.VMEM((tokens, width), jnp.bfloat16),
                pltpu.VMEM((heads, 2, (2 * REACH + 1) * block, hd), jnp.bfloat16),
                pltpu.VMEM((heads, block, hd), jnp.bfloat16),
                pltpu.VMEM((heads, peers, tokens, hd), jnp.bfloat16),
                pltpu.VMEM((heads, peers, tokens, hd), jnp.bfloat16),
                pltpu.VMEM((heads, block, 128), jnp.float32),
                pltpu.VMEM((heads, block, hd), jnp.float32),
                pltpu.VMEM((tiles, 16, SPAN), jnp.float32),
                pltpu.VMEM((heads, block, hd), jnp.bfloat16),
                pltpu.VMEM((tiles, 128), jnp.int32),
                pltpu.VMEM((tiles, 128), jnp.int32),
                pltpu.VMEM((heads, block, hd), jnp.bfloat16),
                pltpu.VMEM((heads, block, hd), jnp.bfloat16),
                pltpu.VMEM((heads, PARTS, 8, 128), jnp.float32),
                pltpu.VMEM((heads, block, hd), jnp.bfloat16),
                pltpu.VMEM((heads, PARTS, 8, 128), jnp.float32),
                dma((3,)), dma((3, heads)), dma((heads,)), dma((heads, 2, peers)),
                dma((heads, 2, 6)), dma((heads, 2, 6)),
                dma((heads, 2, 4)), dma((heads, 2, 4)),
                dma((heads,)), dma((heads,)), dma((2,)),
                dma((heads, PARTS)), dma((heads, PARTS)), dma((heads, PARTS)), dma((heads, PARTS)),
                dma((heads,)), dma((heads,)), dma((heads,)),
            ],
            compiler_params=pltpu.CompilerParams(
                collective_id=0, has_side_effects=True, vmem_limit_bytes=56 * 2 ** 20
            ),
        )(counts.reshape(1, -1), neighbors, queries, keys, values, query_gain.reshape(1, -1), key_gain.reshape(1, -1))

    tokens = P(("cfg", "blk", "uly"), None)
    return jax.shard_map(
        per_device,
        mesh=mesh,
        in_specs=(tokens, tokens, tokens, P(), P(), P("blk", None), P("blk")),
        out_specs=tokens,
        check_vma=False,
    )
```

```python
import functools
import math

import jax
import jax.numpy as jnp
from jax import lax
from jax.experimental import pallas as pl
from jax.experimental.pallas import tpu as pltpu
from jax.sharding import PartitionSpec as P

MESH = pl.DeviceIdType.MESH
TILE = 64
WIDE = 20
FRAME = 60
REACH = 6
GROUP = 2
SPAN = (GROUP + 2) * TILE
NEAR = (-WIDE, 0, WIDE)
AHEAD = (FRAME - WIDE, FRAME, FRAME + WIDE)
PARTS = 4
ROWS = GROUP * TILE


def kernel(
    blocks, peers, heads,
    counts, neighbors, queries_hbm, keys_hbm, values_hbm, query_gain, key_gain,
    out,
    queries, keys, values, kv, queries_in, keys_out, queries_out, total, acc, mask, mixed,
    lists, guest_lists, guests, guest_mixed, guest_total, returned, returned_total,
    load_sem, uly_send, uly_recv, piece_recv, ring_send, ring_recv, pair_send, pair_recv,
    push_send, push_recv, list_sem, return_send, return_recv, total_send, total_recv, back_send, back_recv, own_sem,
):
    tokens = queries.shape[0]
    hd = query_gain.shape[1]
    block = tokens * peers
    tiles = block // TILE
    cfg, me, mine = lax.axis_index("cfg"), lax.axis_index("blk"), lax.axis_index("uly")
    core = lax.rem(me, 2)
    above, below = lax.rem(me + 2, blocks), lax.rem(me + blocks - 2, blocks)
    sibling = me + 1 - 2 * core
    upper = lax.rem(me // 2, 2)
    side = 2 * upper - 1
    partner_blk = me - 2 * side
    outer = lax.rem(me + blocks + 2 * side, blocks)
    outer_sibling = outer + 1 - 2 * core
    gets_half = core == upper
    gives_half = core + upper == 1
    gives_one = core + upper == 2
    gets_one = core - upper == 1
    is_one = core == 1
    scale = hd ** -0.5 * math.log2(math.e)
    own = REACH * block
    units = [(h, which) for h in range(heads) for which in (1, 0)]
    n_units = len(units)

    def slot_row(step):
        return pl.multiple_of(own + step * block, block)

    def at_blk(b):
        return (cfg, b, mine)

    def at_uly(u):
        return (cfg, me, u)

    def partner(d):
        return lax.rem(mine + d, peers)

    barrier = pltpu.get_barrier_semaphore()
    for d in range(1, peers):
        pl.semaphore_signal(barrier, inc=1, device_id=at_uly(partner(d)), device_id_type=MESH)
    for b in (above, below, sibling, outer_sibling):
        pl.semaphore_signal(barrier, inc=1, device_id=at_blk(b), device_id_type=MESH)

    loads = [
        pltpu.make_async_copy(source, target, load_sem.at[i])
        for i, (source, target) in enumerate(((keys_hbm, keys), (values_hbm, values), (queries_hbm, queries)))
    ]
    for load in loads:
        load.start()

    @pl.when(core == 0)
    def _():
        start = pl.multiple_of(own - 5 * block - TILE + upper * (11 * block + TILE), TILE)
        for h, which in units:
            kv[h, which, pl.ds(start, TILE), :] = jnp.zeros((TILE, hd), jnp.bfloat16)

    @pl.when(gets_half)
    def _():
        for h, which in units:
            kv[h, which, pl.ds(slot_row(5 * side), block // 2), :] = jnp.zeros((block // 2, hd), jnp.bfloat16)

    def columns(u, h):
        return pl.ds(pl.multiple_of((u * heads + h) * hd, hd), hd)

    def rows_of(start, u):
        return pl.ds(pl.multiple_of(start + u * tokens, tokens), tokens)

    def normed(states, gain, u, h):
        wide = states[:, columns(u, h)].astype(jnp.float32)
        factor = lax.rsqrt(jnp.mean(wide * wide, axis=-1, keepdims=True) + 1e-06)
        return (wide * factor * gain[...]).astype(jnp.bfloat16)

    def norm(kind, h):
        states, gain, target = (queries, query_gain, queries_out) if kind == 2 else (keys, key_gain, keys_out)

        def one(u, carry):
            target[h, u] = normed(states, gain, u, h)
            return carry

        lax.fori_loop(0, peers, one, 0)

    def spread(kind, h):
        if kind == 2:
            landing = queries_in.at[h, rows_of(0, mine), :]
            queries_in[h, rows_of(0, mine), :] = queries_out[h, mine]
        else:
            landing = kv.at[h, kind, rows_of(own, mine), :]

        def send(d, carry):
            u = partner(d)
            if kind == 2:
                source = queries_out.at[h, u]
            elif kind == 1:
                source = values.at[:, columns(u, h)]
            else:
                source = keys_out.at[h, u]
            arrival = uly_recv.at[h] if kind == 2 else piece_recv.at[h, kind, d]
            pltpu.make_async_remote_copy(
                source, landing, uly_send.at[kind, h], arrival, device_id=at_uly(u), device_id_type=MESH,
            ).start()
            return carry

        lax.fori_loop(1, peers, send, 0)

    rest = (peers - 1) * tokens

    def wait_bytes(ref, sem):
        pltpu.make_async_copy(ref, ref, sem).wait()

    sent = []

    def copy_to(source, target, send, recv, b):
        copy = pltpu.make_async_remote_copy(
            source, target, send, recv, device_id=at_blk(b), device_id_type=MESH
        )
        copy.start()
        sent.append(copy)
        return copy

    def block_of(unit, step):
        return kv.at[(*unit, pl.ds(slot_row(step), block), slice(None))]

    def ring(unit, slot, source, target, to):
        return copy_to(
            block_of(unit, source), block_of(unit, target), ring_send.at[(*unit, slot)], ring_recv.at[(*unit, slot)], to
        )

    def share(unit, slot, step):
        return copy_to(
            block_of(unit, step), block_of(unit, step + 2 * core - 1),
            pair_send.at[(*unit, slot)], pair_recv.at[(*unit, slot)], sibling,
        )

    def half_of(unit, step):
        return kv.at[(*unit, pl.ds(pl.multiple_of(slot_row(step) + block // 2, block // 2), block // 2), slice(None))]

    def tile_of(unit, step, tile):
        return kv.at[(*unit, pl.ds(pl.multiple_of(slot_row(step) + tile * TILE, TILE), TILE), slice(None))]

    def copy_if(flag, unit, slot, source, target, to):
        @pl.when(flag)
        def _():
            pltpu.make_async_remote_copy(
                source, target, ring_send.at[(*unit, slot)], ring_recv.at[(*unit, slot)],
                device_id=at_blk(to), device_id_type=MESH,
            ).start()

    def wait_if(flag, sem, rows):
        @pl.when(flag)
        def _():
            wait_bytes(kv.at[0, 0, pl.ds(own, rows), :], sem)

    ringed, shared = {}, {}

    def forward(unit, u):
        h, which = unit
        for slot, target, to in ((0, own - 2 * block, above), (1, own + 2 * block, below)):
            pltpu.make_async_remote_copy(
                kv.at[h, which, rows_of(own, u), :], kv.at[h, which, rows_of(target, u), :],
                ring_send.at[h, which, slot], ring_recv.at[h, which, slot],
                device_id=at_blk(to), device_id_type=MESH,
            ).start()

    def store_own(unit):
        h, which = unit
        kv[h, which, rows_of(own, mine), :] = keys_out[h, mine] if which == 0 else values[:, columns(mine, h)]

    def step_own(k):
        if k >= n_units:
            return
        h, which = unit = units[k]

        def one(d, carry):
            u = lax.rem(mine + peers - d, peers)
            wait_bytes(kv.at[h, which, rows_of(own, u), :], piece_recv.at[h, which, d])
            forward(unit, u)
            return carry

        lax.fori_loop(1, peers, one, 0)
        for slot, target, to in ((0, -2, above), (1, 2, below)):
            ringed[k, slot] = pltpu.make_async_remote_copy(
                block_of(unit, 0), block_of(unit, target), ring_send.at[h, which, slot], ring_recv.at[h, which, slot],
                device_id=at_blk(to), device_id_type=MESH,
            )
            sent.append(ringed[k, slot])
        shared[k, 0] = share(unit, 0, 0)

    def step_next(n):
        unit = units[n]
        ringed[n, 0].wait_recv()
        ringed[n, 1].wait_recv()
        ringed[n, 2] = ring(unit, 2, -2 * side, -4 * side, outer)
        copy_if(gives_half, unit, 3, half_of(unit, 2 * side), half_of(unit, 4 * side), partner_blk)
        copy_if(gives_one, unit, 3, tile_of(unit, 2, 0), tile_of(unit, 4, 0), partner_blk)
        shared[n, 1] = share(unit, 1, -2)
        shared[n, 2] = share(unit, 2, 2)

    def step_second(n):
        ringed[n, 2].wait_recv()
        shared[n, 3] = share(units[n], 3, 4 * side)

    def step_far(n):
        unit = units[n]
        last_tile = upper * (tiles - 1)
        wait_if(gets_half, ring_recv.at[(*unit, 3)], block // 2)
        wait_if(gets_one, ring_recv.at[(*unit, 3)], TILE)
        copy_if(
            gets_half, unit, 4, half_of(unit, -4 * side), half_of(unit, 2 * core - 1 - 6 * side), outer_sibling
        )
        copy_if(is_one, unit, 5, tile_of(unit, -4 * side, last_tile), tile_of(unit, -6 * side, last_tile), outer)

    def push(h):
        wait_bytes(queries_in.at[h, pl.ds(0, rest), :], uly_recv.at[h])
        pushed[h] = copy_to(queries_in.at[h], guests.at[h], push_send.at[h], push_recv.at[h], partner_blk)

    pushed = {}

    def list_tiles():
        shape = neighbors.shape
        row = lax.broadcasted_iota(jnp.int32, shape, 0)
        count = jnp.zeros(shape, jnp.int32)
        for t in range(tiles):
            count = jnp.where(row == t, counts[0, t], count)
        live = lax.broadcasted_iota(jnp.int32, shape, 1) < count
        lists[...] = jnp.full(lists.shape, -(2 ** 20), jnp.int32)
        lists[:, : shape[1]] = jnp.where(live, neighbors[...], -(2 ** 20))

    def build_mask(first, centres, entries, blk):
        shape = (tiles, SPAN)
        row = lax.broadcasted_iota(jnp.int32, shape, 0)
        place = lax.broadcasted_iota(jnp.int32, shape, 1) // TILE
        base = blk * tiles + row - 1 - lax.rem(row, GROUP) + place
        listed = entries[...]
        for i, centre in enumerate(centres):
            live = jnp.zeros(shape, jnp.float32)
            for n in range(neighbors.shape[1]):
                live = jnp.where(base + centre == listed[:, n : n + 1], 1.0, live)
            for t in range(tiles):
                mask[t, first + i : first + i + 1, :] = live[t : t + 1, :]

    def windows_sum(h, t, q, windows, sums, result):
        def near(centre):
            return pl.ds(pl.multiple_of(own + (t + centre - 1) * TILE, TILE), SPAN)

        def score(centre):
            return lax.dot_general(
                q, kv[h, 0, near(centre), :], (((1,), (1,)), ((), ())), preferred_element_type=jnp.float32
            )

        scores = score(windows[0][0])
        for i, (centre, line) in enumerate(windows):
            coming = score(windows[i + 1][0]) if i + 1 < len(windows) else None
            live = jnp.concatenate(
                [jnp.broadcast_to(mask[t + a, line : line + 1, :], (TILE, SPAN)) for a in range(GROUP)], axis=0
            )
            weights = jnp.exp2(scores * scale) * live
            for part in range(0, SPAN, 128):
                sums = sums + weights[:, part : part + 128]
            result = result + jnp.dot(
                weights.astype(jnp.bfloat16), kv[h, 1, near(centre), :], preferred_element_type=jnp.float32
            )
            scores = coming
        return sums, result

    def over_groups(work, begin=0, end=PARTS):
        each = tiles // GROUP // PARTS

        def part(i, carry):
            for s in range(each):
                t = (i * each + s) * GROUP
                work(i, s, t, pl.ds(pl.multiple_of(t * TILE, ROWS), ROWS))
            return carry

        lax.fori_loop(begin, end, part, 0)

    zeros = functools.partial(jnp.zeros, dtype=jnp.float32)

    def home(h):
        for which in (1, 0):
            for slot in (0, 1, 2):
                shared[units.index((h, which)), slot].wait_recv()

        def work(i, s, t, rows):
            windows = [(centre, line) for line, centre in enumerate(NEAR)]
            total[h, rows, :], acc[h, rows, :] = windows_sum(
                h, t, queries_in[h, rows, :], windows, zeros((ROWS, 128)), zeros((ROWS, hd))
            )

        over_groups(work)

    def diagonal():
        return lax.broadcasted_iota(jnp.int32, (ROWS, 128), 0) == lax.broadcasted_iota(jnp.int32, (ROWS, 128), 1)

    return_copies = {}

    def guest(h):
        for which in (1, 0):
            shared[units.index((h, which)), 3].wait_recv()
        pushed[h].wait_recv()

        def work(i, s, t, rows):
            windows = [(side * (ahead - 2 * tiles), 6 + j) for j, ahead in enumerate(AHEAD)]
            sums, result = windows_sum(h, t, guests[h, rows, :], windows, zeros((ROWS, 128)), zeros((ROWS, hd)))
            guest_mixed[h, rows, :] = result.astype(jnp.bfloat16)
            column = jnp.sum(sums, axis=-1, keepdims=True)
            guest_total[h, i, s : s + 1, :] = jnp.sum(jnp.where(diagonal(), column, 0.0), axis=0, keepdims=True)

        for i in range(PARTS):
            over_groups(work, i, i + 1)
            rows = pl.ds(i * (block // PARTS), block // PARTS)
            return_copies[h, i, 0] = copy_to(
                guest_mixed.at[h, rows, :], returned.at[h, rows, :], return_send.at[h, i], return_recv.at[h, i], partner_blk
            )
            return_copies[h, i, 1] = copy_to(
                guest_total.at[h, i], returned_total.at[h, i], total_send.at[h, i], total_recv.at[h, i], partner_blk
            )

    def middle(h):
        def work(i, s, t, rows):
            windows = [(side * ahead, 3 + j) for j, ahead in enumerate(AHEAD[:2])]
            total[h, rows, :], acc[h, rows, :] = windows_sum(
                h, t, queries_in[h, rows, :], windows, total[h, rows, :], acc[h, rows, :]
            )

        over_groups(work)

    def finish(h):
        def wait_far(flag, slot, rows):
            for which in (1, 0):
                wait_if(flag, ring_recv.at[h, which, slot], rows)

        def work(i, s, t, rows):
            sums, result = windows_sum(
                h, t, queries_in[h, rows, :], [(side * AHEAD[2], 5)], total[h, rows, :], acc[h, rows, :]
            )
            line = returned_total[h, i, s : s + 1, :]
            sums = sums + jnp.where(diagonal(), jnp.broadcast_to(line, (ROWS, 128)), 0.0)
            result = result + returned[h, rows, :].astype(jnp.float32)
            mixed[h, rows, :] = (result / jnp.sum(sums, axis=-1, keepdims=True)).astype(jnp.bfloat16)

        each = peers // PARTS
        for i in range(PARTS):
            return_copies[h, i, 0].wait_recv()
            return_copies[h, i, 1].wait_recv()
            if i == 0:
                wait_far(gets_one, 5, TILE)
            if i == 1:
                wait_far(gets_half, 4, block // 2)
            if i == PARTS - 1:
                wait_far(gives_one, 5, TILE)
            over_groups(work, i, i + 1)
            for u in range(i * each, (i + 1) * each):
                send_back(h, u)

    def send_back(h, u):
        source = mixed.at[h, rows_of(0, u), :]
        landing = out.at[:, columns(mine, h)]

        @pl.when(u != mine)
        def _():
            pltpu.make_async_remote_copy(
                source, landing, back_send.at[h], back_recv.at[h], device_id=at_uly(u), device_id_type=MESH,
            ).start()

        @pl.when(u == mine)
        def _():
            pltpu.make_async_copy(source, landing, own_sem.at[h]).start()

    loads[0].wait()
    norm(0, 0)
    store_own((0, 0))
    loads[1].wait()
    store_own((0, 1))
    pl.semaphore_wait(barrier, 4 + peers - 1)
    forward((0, 1), mine)
    spread(1, 0)
    forward((0, 0), mine)
    spread(0, 0)
    for h in range(1, heads):
        store_own((h, 1))
        forward((h, 1), mine)
    step_own(0)
    norm(0, 1)
    store_own((1, 0))
    forward((1, 0), mine)
    spread(1, 1)
    spread(0, 1)
    step_own(1)
    loads[2].wait()
    norm(2, 0)
    spread(2, 0)
    for h in range(2, heads):
        norm(0, h)
        store_own((h, 0))
        forward((h, 0), mine)
        spread(1, h)
        spread(0, h)
    step_next(0)
    for h in range(1, heads):
        norm(2, h)
        spread(2, h)
    list_tiles()
    lists_copy = copy_to(lists, guest_lists, list_sem.at[0], list_sem.at[1], partner_blk)
    guest_total[...] = jnp.zeros(guest_total.shape, jnp.float32)
    step_own(2)
    push(0)
    step_next(1)
    step_second(0)
    build_mask(0, NEAR, lists, me)
    step_own(3)
    step_next(2)
    step_second(1)
    push(1)
    home(0)
    build_mask(3, [side * ahead for ahead in AHEAD], lists, me)
    lists_copy.wait_recv()
    build_mask(6, [side * ahead for ahead in AHEAD], guest_lists, partner_blk)
    step_own(4)
    step_next(3)
    step_second(2)
    push(2)
    guest(0)
    middle(0)
    step_own(5)
    step_next(4)
    step_far(0)
    step_far(1)
    step_second(3)
    home(1)
    step_next(5)
    step_far(2)
    step_far(3)
    step_far(4)
    guest(1)
    step_second(4)
    middle(1)
    finish(0)
    home(2)
    step_far(5)
    step_second(5)
    guest(2)
    finish(1)
    middle(2)
    finish(2)

    for copy in sent:
        copy.wait_send()
    for unit in units:
        wait_if(gives_half, ring_send.at[(*unit, 3)], block // 2)
        wait_if(gives_one, ring_send.at[(*unit, 3)], TILE)
        wait_if(gets_half, ring_send.at[(*unit, 4)], block // 2)
        wait_if(is_one, ring_send.at[(*unit, 5)], TILE)
    for h in range(heads):
        for kind in range(3):
            wait_bytes(queries_in.at[h, pl.ds(0, rest), :], uly_send.at[kind, h])
        wait_bytes(queries_in.at[h, pl.ds(0, rest), :], back_send.at[h])
        wait_bytes(queries_in.at[h, pl.ds(0, tokens), :], own_sem.at[h])
    for h in range(heads):
        wait_bytes(queries_in.at[h, pl.ds(0, rest), :], back_recv.at[h])


def solution(mesh):
    blocks, peers = mesh.shape["blk"], mesh.shape["uly"]

    def per_device(queries, keys, values, query_gain, key_gain, neighbors, counts):
        tokens, width = queries.shape
        hd = query_gain.shape[0]
        heads = width // hd // peers
        block = tokens * peers
        tiles = block // TILE
        vmem = pl.BlockSpec(memory_space=pltpu.VMEM)
        smem = pl.BlockSpec(memory_space=pltpu.SMEM)
        dma = pltpu.SemaphoreType.DMA
        return pl.pallas_call(
            functools.partial(kernel, blocks, peers, heads),
            out_shape=jax.ShapeDtypeStruct((tokens, width), jnp.bfloat16),
            in_specs=[smem, vmem] + [pl.BlockSpec(memory_space=pl.ANY)] * 3 + [vmem] * 2,
            out_specs=pl.BlockSpec(memory_space=pl.ANY),
            scratch_shapes=[
                pltpu.VMEM((tokens, width), jnp.bfloat16),
                pltpu.VMEM((tokens, width), jnp.bfloat16),
                pltpu.VMEM((tokens, width), jnp.bfloat16),
                pltpu.VMEM((heads, 2, (2 * REACH + 1) * block, hd), jnp.bfloat16),
                pltpu.VMEM((heads, block, hd), jnp.bfloat16),
                pltpu.VMEM((heads, peers, tokens, hd), jnp.bfloat16),
                pltpu.VMEM((heads, peers, tokens, hd), jnp.bfloat16),
                pltpu.VMEM((heads, block, 128), jnp.float32),
                pltpu.VMEM((heads, block, hd), jnp.float32),
                pltpu.VMEM((tiles, 16, SPAN), jnp.float32),
                pltpu.VMEM((heads, block, hd), jnp.bfloat16),
                pltpu.VMEM((tiles, 128), jnp.int32),
                pltpu.VMEM((tiles, 128), jnp.int32),
                pltpu.VMEM((heads, block, hd), jnp.bfloat16),
                pltpu.VMEM((heads, block, hd), jnp.bfloat16),
                pltpu.VMEM((heads, PARTS, 8, 128), jnp.float32),
                pltpu.VMEM((heads, block, hd), jnp.bfloat16),
                pltpu.VMEM((heads, PARTS, 8, 128), jnp.float32),
                dma((3,)), dma((3, heads)), dma((heads,)), dma((heads, 2, peers)),
                dma((heads, 2, 6)), dma((heads, 2, 6)),
                dma((heads, 2, 4)), dma((heads, 2, 4)),
                dma((heads,)), dma((heads,)), dma((2,)),
                dma((heads, PARTS)), dma((heads, PARTS)), dma((heads, PARTS)), dma((heads, PARTS)),
                dma((heads,)), dma((heads,)), dma((heads,)),
            ],
            compiler_params=pltpu.CompilerParams(
                collective_id=0, has_side_effects=True, vmem_limit_bytes=56 * 2 ** 20
            ),
        )(counts.reshape(1, -1), neighbors, queries, keys, values, query_gain.reshape(1, -1), key_gain.reshape(1, -1))

    tokens = P(("cfg", "blk", "uly"), None)
    return jax.shard_map(
        per_device,
        mesh=mesh,
        in_specs=(tokens, tokens, tokens, P(), P(), P("blk", None), P("blk")),
        out_specs=tokens,
        check_vma=False,
    )
```

```python
import functools
import math

import jax
import jax.numpy as jnp
from jax import lax
from jax.experimental import pallas as pl
from jax.experimental.pallas import tpu as pltpu
from jax.sharding import PartitionSpec as P

MESH = pl.DeviceIdType.MESH
TILE = 64
WIDE = 20
FRAME = 60
REACH = 6
GROUP = 2
SPAN = (GROUP + 2) * TILE
NEAR = (-WIDE, 0, WIDE)
AHEAD = (FRAME - WIDE, FRAME, FRAME + WIDE)
PARTS = 4
ROWS = GROUP * TILE


def kernel(
    blocks, peers, heads,
    counts, neighbors, queries_hbm, keys_hbm, values_hbm, query_gain, key_gain,
    out,
    queries, keys, values, kv, queries_in, keys_out, queries_out, total, acc, mask, mixed,
    lists, guest_lists, guests, guest_mixed, guest_total, returned, returned_total,
    load_sem, uly_send, uly_recv, piece_recv, ring_send, ring_recv, pair_send, pair_recv,
    push_send, push_recv, list_sem, return_send, return_recv, total_send, total_recv, back_send, back_recv, own_sem,
):
    tokens = queries.shape[0]
    hd = query_gain.shape[1]
    block = tokens * peers
    tiles = block // TILE
    cfg, me, mine = lax.axis_index("cfg"), lax.axis_index("blk"), lax.axis_index("uly")
    core = lax.rem(me, 2)
    above, below = lax.rem(me + 2, blocks), lax.rem(me + blocks - 2, blocks)
    sibling = me + 1 - 2 * core
    upper = lax.rem(me // 2, 2)
    side = 2 * upper - 1
    partner_blk = me - 2 * side
    outer = lax.rem(me + blocks + 2 * side, blocks)
    outer_sibling = outer + 1 - 2 * core
    gets_half = core == upper
    gives_half = core + upper == 1
    gives_one = core + upper == 2
    gets_one = core - upper == 1
    is_one = core == 1
    scale = hd ** -0.5 * math.log2(math.e)
    own = REACH * block
    units = [(h, which) for h in range(heads) for which in (1, 0)]
    n_units = len(units)

    def slot_row(step):
        return pl.multiple_of(own + step * block, block)

    def at_blk(b):
        return (cfg, b, mine)

    def at_uly(u):
        return (cfg, me, u)

    def partner(d):
        return lax.rem(mine + d, peers)

    barrier = pltpu.get_barrier_semaphore()
    for d in range(1, peers):
        pl.semaphore_signal(barrier, inc=1, device_id=at_uly(partner(d)), device_id_type=MESH)
    for b in (above, below, sibling, outer_sibling):
        pl.semaphore_signal(barrier, inc=1, device_id=at_blk(b), device_id_type=MESH)

    loads = [
        pltpu.make_async_copy(source, target, load_sem.at[i])
        for i, (source, target) in enumerate(((keys_hbm, keys), (values_hbm, values), (queries_hbm, queries)))
    ]
    for load in loads:
        load.start()

    @pl.when(core == 0)
    def _():
        start = pl.multiple_of(own - 5 * block - TILE + upper * (11 * block + TILE), TILE)
        for h, which in units:
            kv[h, which, pl.ds(start, TILE), :] = jnp.zeros((TILE, hd), jnp.bfloat16)

    @pl.when(gets_half)
    def _():
        for h, which in units:
            kv[h, which, pl.ds(slot_row(5 * side), block // 2), :] = jnp.zeros((block // 2, hd), jnp.bfloat16)

    def columns(u, h):
        return pl.ds(pl.multiple_of((u * heads + h) * hd, hd), hd)

    def rows_of(start, u):
        return pl.ds(pl.multiple_of(start + u * tokens, tokens), tokens)

    def normed(states, gain, u, h):
        wide = states[:, columns(u, h)].astype(jnp.float32)
        factor = lax.rsqrt(jnp.mean(wide * wide, axis=-1, keepdims=True) + 1e-06)
        return (wide * factor * gain[...]).astype(jnp.bfloat16)

    def norm(kind, h):
        states, gain, target = (queries, query_gain, queries_out) if kind == 2 else (keys, key_gain, keys_out)

        def one(u, carry):
            target[h, u] = normed(states, gain, u, h)
            return carry

        lax.fori_loop(0, peers, one, 0)

    def spread(kind, h):
        if kind == 2:
            landing = queries_in.at[h, rows_of(0, mine), :]
            queries_in[h, rows_of(0, mine), :] = queries_out[h, mine]
        else:
            landing = kv.at[h, kind, rows_of(own, mine), :]

        def send(d, carry):
            u = partner(d)
            if kind == 2:
                source = queries_out.at[h, u]
            elif kind == 1:
                source = values.at[:, columns(u, h)]
            else:
                source = keys_out.at[h, u]
            arrival = uly_recv.at[h] if kind == 2 else piece_recv.at[h, kind, d]
            pltpu.make_async_remote_copy(
                source, landing, uly_send.at[kind, h], arrival, device_id=at_uly(u), device_id_type=MESH,
            ).start()
            return carry

        lax.fori_loop(1, peers, send, 0)

    rest = (peers - 1) * tokens

    def wait_bytes(ref, sem):
        pltpu.make_async_copy(ref, ref, sem).wait()

    sent = []

    def copy_to(source, target, send, recv, b):
        copy = pltpu.make_async_remote_copy(
            source, target, send, recv, device_id=at_blk(b), device_id_type=MESH
        )
        copy.start()
        sent.append(copy)
        return copy

    def block_of(unit, step):
        return kv.at[(*unit, pl.ds(slot_row(step), block), slice(None))]

    def ring(unit, slot, source, target, to):
        return copy_to(
            block_of(unit, source), block_of(unit, target), ring_send.at[(*unit, slot)], ring_recv.at[(*unit, slot)], to
        )

    def share(unit, slot, step):
        return copy_to(
            block_of(unit, step), block_of(unit, step + 2 * core - 1),
            pair_send.at[(*unit, slot)], pair_recv.at[(*unit, slot)], sibling,
        )

    def part_of(unit, step, i):
        start = pl.multiple_of(slot_row(step) + i * (block // 2), block // 2)
        return kv.at[(*unit, pl.ds(start, block // 2), slice(None))]

    def half_of(unit, step):
        return kv.at[(*unit, pl.ds(pl.multiple_of(slot_row(step) + block // 2, block // 2), block // 2), slice(None))]

    def tile_of(unit, step, tile):
        return kv.at[(*unit, pl.ds(pl.multiple_of(slot_row(step) + tile * TILE, TILE), TILE), slice(None))]

    def copy_if(flag, unit, slot, source, target, to):
        @pl.when(flag)
        def _():
            pltpu.make_async_remote_copy(
                source, target, ring_send.at[(*unit, slot)], ring_recv.at[(*unit, slot)],
                device_id=at_blk(to), device_id_type=MESH,
            ).start()

    def wait_if(flag, sem, rows):
        @pl.when(flag)
        def _():
            wait_bytes(kv.at[0, 0, pl.ds(own, rows), :], sem)

    ringed, shared = {}, {}

    def forward(unit, u):
        h, which = unit
        for slot, target, to in ((0, own - 2 * block, above), (1, own + 2 * block, below)):
            pltpu.make_async_remote_copy(
                kv.at[h, which, rows_of(own, u), :], kv.at[h, which, rows_of(target, u), :],
                ring_send.at[h, which, slot], ring_recv.at[h, which, slot],
                device_id=at_blk(to), device_id_type=MESH,
            ).start()

    def store_own(unit):
        h, which = unit
        kv[h, which, rows_of(own, mine), :] = keys_out[h, mine] if which == 0 else values[:, columns(mine, h)]

    def step_own(k):
        if k >= n_units:
            return
        h, which = unit = units[k]

        def one(d, carry):
            u = lax.rem(mine + peers - d, peers)
            wait_bytes(kv.at[h, which, rows_of(own, u), :], piece_recv.at[h, which, d])
            forward(unit, u)
            return carry

        lax.fori_loop(1, peers, one, 0)
        for slot, target, to in ((0, -2, above), (1, 2, below)):
            ringed[k, slot] = pltpu.make_async_remote_copy(
                block_of(unit, 0), block_of(unit, target), ring_send.at[h, which, slot], ring_recv.at[h, which, slot],
                device_id=at_blk(to), device_id_type=MESH,
            )
            sent.append(ringed[k, slot])
        shared[k, 0] = share(unit, 0, 0)

    def step_next(n):
        unit = units[n]
        ringed[n, 0].wait_recv()
        ringed[n, 1].wait_recv()
        if n == n_units - 1:
            for i, slot in enumerate((2, 6)):
                ringed[n, slot] = copy_to(
                    part_of(unit, -2 * side, i), part_of(unit, -4 * side, i),
                    ring_send.at[(*unit, slot)], ring_recv.at[(*unit, slot)], outer,
                )
        else:
            ringed[n, 2] = ring(unit, 2, -2 * side, -4 * side, outer)
        copy_if(gives_half, unit, 3, half_of(unit, 2 * side), half_of(unit, 4 * side), partner_blk)
        copy_if(gives_one, unit, 3, tile_of(unit, 2, 0), tile_of(unit, 4, 0), partner_blk)
        shared[n, 1] = share(unit, 1, -2)
        shared[n, 2] = share(unit, 2, 2)

    def step_second(n):
        unit = units[n]
        ringed[n, 2].wait_recv()
        if n < n_units - 1:
            shared[n, 3] = share(unit, 3, 4 * side)
            return
        for i, slot in enumerate((3, 4)):
            if i == 1:
                ringed[n, 6].wait_recv()
            shared[n, slot] = copy_to(
                part_of(unit, 4 * side, i), part_of(unit, 4 * side + 2 * core - 1, i),
                pair_send.at[(*unit, slot)], pair_recv.at[(*unit, slot)], sibling,
            )

    def step_far(n):
        unit = units[n]
        last_tile = upper * (tiles - 1)
        wait_if(gets_half, ring_recv.at[(*unit, 3)], block // 2)
        wait_if(gets_one, ring_recv.at[(*unit, 3)], TILE)
        copy_if(
            gets_half, unit, 4, half_of(unit, -4 * side), half_of(unit, 2 * core - 1 - 6 * side), outer_sibling
        )
        copy_if(is_one, unit, 5, tile_of(unit, -4 * side, last_tile), tile_of(unit, -6 * side, last_tile), outer)

    def push(h):
        wait_bytes(queries_in.at[h, pl.ds(0, rest), :], uly_recv.at[h])
        pushed[h] = copy_to(queries_in.at[h], guests.at[h], push_send.at[h], push_recv.at[h], partner_blk)

    pushed = {}

    def list_tiles():
        shape = neighbors.shape
        row = lax.broadcasted_iota(jnp.int32, shape, 0)
        count = jnp.zeros(shape, jnp.int32)
        for t in range(tiles):
            count = jnp.where(row == t, counts[0, t], count)
        live = lax.broadcasted_iota(jnp.int32, shape, 1) < count
        lists[...] = jnp.full(lists.shape, -(2 ** 20), jnp.int32)
        lists[:, : shape[1]] = jnp.where(live, neighbors[...], -(2 ** 20))

    def build_mask(first, centres, entries, blk):
        shape = (tiles, SPAN)
        row = lax.broadcasted_iota(jnp.int32, shape, 0)
        place = lax.broadcasted_iota(jnp.int32, shape, 1) // TILE
        base = blk * tiles + row - 1 - lax.rem(row, GROUP) + place
        listed = entries[...]
        for i, centre in enumerate(centres):
            live = jnp.zeros(shape, jnp.float32)
            for n in range(neighbors.shape[1]):
                live = jnp.where(base + centre == listed[:, n : n + 1], 1.0, live)
            for t in range(tiles):
                mask[t, first + i : first + i + 1, :] = live[t : t + 1, :]

    def windows_sum(h, t, q, windows, sums, result):
        def near(centre):
            return pl.ds(pl.multiple_of(own + (t + centre - 1) * TILE, TILE), SPAN)

        def score(centre):
            return lax.dot_general(
                q, kv[h, 0, near(centre), :], (((1,), (1,)), ((), ())), preferred_element_type=jnp.float32
            )

        scores = score(windows[0][0])
        for i, (centre, line) in enumerate(windows):
            coming = score(windows[i + 1][0]) if i + 1 < len(windows) else None
            live = jnp.concatenate(
                [jnp.broadcast_to(mask[t + a, line : line + 1, :], (TILE, SPAN)) for a in range(GROUP)], axis=0
            )
            weights = jnp.exp2(scores * scale) * live
            for part in range(0, SPAN, 128):
                sums = sums + weights[:, part : part + 128]
            result = result + jnp.dot(
                weights.astype(jnp.bfloat16), kv[h, 1, near(centre), :], preferred_element_type=jnp.float32
            )
            scores = coming
        return sums, result

    def over_groups(work, begin=0, end=PARTS):
        each = tiles // GROUP // PARTS

        def part(i, carry):
            for s in range(each):
                t = (i * each + s) * GROUP
                work(i, s, t, pl.ds(pl.multiple_of(t * TILE, ROWS), ROWS))
            return carry

        lax.fori_loop(begin, end, part, 0)

    zeros = functools.partial(jnp.zeros, dtype=jnp.float32)

    def home(h):
        for which in (1, 0):
            for slot in (0, 1, 2):
                shared[units.index((h, which)), slot].wait_recv()

        def work(i, s, t, rows):
            windows = [(centre, line) for line, centre in enumerate(NEAR)]
            total[h, rows, :], acc[h, rows, :] = windows_sum(
                h, t, queries_in[h, rows, :], windows, zeros((ROWS, 128)), zeros((ROWS, hd))
            )

        over_groups(work)

    def diagonal():
        return lax.broadcasted_iota(jnp.int32, (ROWS, 128), 0) == lax.broadcasted_iota(jnp.int32, (ROWS, 128), 1)

    return_copies = {}

    def guest(h):
        for which in (1, 0):
            for slot in (3, 4):
                if (units.index((h, which)), slot) in shared:
                    shared[units.index((h, which)), slot].wait_recv()
        pushed[h].wait_recv()

        def work(i, s, t, rows):
            windows = [(side * (ahead - 2 * tiles), 6 + j) for j, ahead in enumerate(AHEAD)]
            sums, result = windows_sum(h, t, guests[h, rows, :], windows, zeros((ROWS, 128)), zeros((ROWS, hd)))
            guest_mixed[h, rows, :] = result.astype(jnp.bfloat16)
            column = jnp.sum(sums, axis=-1, keepdims=True)
            guest_total[h, i, s : s + 1, :] = jnp.sum(jnp.where(diagonal(), column, 0.0), axis=0, keepdims=True)

        for i in range(PARTS):
            over_groups(work, i, i + 1)
            rows = pl.ds(i * (block // PARTS), block // PARTS)
            return_copies[h, i, 0] = copy_to(
                guest_mixed.at[h, rows, :], returned.at[h, rows, :], return_send.at[h, i], return_recv.at[h, i], partner_blk
            )
            return_copies[h, i, 1] = copy_to(
                guest_total.at[h, i], returned_total.at[h, i], total_send.at[h, i], total_recv.at[h, i], partner_blk
            )

    def middle(h):
        def work(i, s, t, rows):
            windows = [(side * ahead, 3 + j) for j, ahead in enumerate(AHEAD[:2])]
            total[h, rows, :], acc[h, rows, :] = windows_sum(
                h, t, queries_in[h, rows, :], windows, total[h, rows, :], acc[h, rows, :]
            )

        over_groups(work)

    def finish(h):
        def wait_far(flag, slot, rows):
            for which in (1, 0):
                wait_if(flag, ring_recv.at[h, which, slot], rows)

        def work(i, s, t, rows):
            sums, result = windows_sum(
                h, t, queries_in[h, rows, :], [(side * AHEAD[2], 5)], total[h, rows, :], acc[h, rows, :]
            )
            line = returned_total[h, i, s : s + 1, :]
            sums = sums + jnp.where(diagonal(), jnp.broadcast_to(line, (ROWS, 128)), 0.0)
            result = result + returned[h, rows, :].astype(jnp.float32)
            mixed[h, rows, :] = (result / jnp.sum(sums, axis=-1, keepdims=True)).astype(jnp.bfloat16)

        each = peers // PARTS
        for i in range(PARTS):
            return_copies[h, i, 0].wait_recv()
            return_copies[h, i, 1].wait_recv()
            if i == 0:
                wait_far(gets_one, 5, TILE)
            if i == 1:
                wait_far(gets_half, 4, block // 2)
            if i == PARTS - 1:
                wait_far(gives_one, 5, TILE)
            over_groups(work, i, i + 1)
            for u in range(i * each, (i + 1) * each):
                send_back(h, u)

    def send_back(h, u):
        source = mixed.at[h, rows_of(0, u), :]
        landing = out.at[:, columns(mine, h)]

        @pl.when(u != mine)
        def _():
            pltpu.make_async_remote_copy(
                source, landing, back_send.at[h], back_recv.at[h], device_id=at_uly(u), device_id_type=MESH,
            ).start()

        @pl.when(u == mine)
        def _():
            pltpu.make_async_copy(source, landing, own_sem.at[h]).start()

    loads[0].wait()
    norm(0, 0)
    store_own((0, 0))
    loads[1].wait()
    store_own((0, 1))
    pl.semaphore_wait(barrier, 4 + peers - 1)
    forward((0, 1), mine)
    spread(1, 0)
    forward((0, 0), mine)
    spread(0, 0)
    for h in range(1, heads):
        store_own((h, 1))
        forward((h, 1), mine)
    step_own(0)
    norm(0, 1)
    store_own((1, 0))
    forward((1, 0), mine)
    spread(1, 1)
    spread(0, 1)
    step_own(1)
    loads[2].wait()
    norm(2, 0)
    spread(2, 0)
    for h in range(2, heads):
        norm(0, h)
        store_own((h, 0))
        forward((h, 0), mine)
        spread(1, h)
        spread(0, h)
    step_next(0)
    for h in range(1, heads):
        norm(2, h)
        spread(2, h)
    list_tiles()
    lists_copy = copy_to(lists, guest_lists, list_sem.at[0], list_sem.at[1], partner_blk)
    guest_total[...] = jnp.zeros(guest_total.shape, jnp.float32)
    step_own(2)
    push(0)
    step_next(1)
    step_second(0)
    build_mask(0, NEAR, lists, me)
    step_own(3)
    step_next(2)
    step_second(1)
    push(1)
    home(0)
    build_mask(3, [side * ahead for ahead in AHEAD], lists, me)
    lists_copy.wait_recv()
    build_mask(6, [side * ahead for ahead in AHEAD], guest_lists, partner_blk)
    step_own(4)
    step_next(3)
    step_second(2)
    push(2)
    guest(0)
    middle(0)
    step_own(5)
    step_next(4)
    step_far(0)
    step_far(1)
    step_second(3)
    home(1)
    step_next(5)
    step_far(2)
    step_far(3)
    step_far(4)
    guest(1)
    step_second(4)
    middle(1)
    finish(0)
    home(2)
    step_far(5)
    step_second(5)
    guest(2)
    finish(1)
    middle(2)
    finish(2)

    for copy in sent:
        copy.wait_send()
    for unit in units:
        wait_if(gives_half, ring_send.at[(*unit, 3)], block // 2)
        wait_if(gives_one, ring_send.at[(*unit, 3)], TILE)
        wait_if(gets_half, ring_send.at[(*unit, 4)], block // 2)
        wait_if(is_one, ring_send.at[(*unit, 5)], TILE)
    for h in range(heads):
        for kind in range(3):
            wait_bytes(queries_in.at[h, pl.ds(0, rest), :], uly_send.at[kind, h])
        wait_bytes(queries_in.at[h, pl.ds(0, rest), :], back_send.at[h])
        wait_bytes(queries_in.at[h, pl.ds(0, tokens), :], own_sem.at[h])
    for h in range(heads):
        wait_bytes(queries_in.at[h, pl.ds(0, rest), :], back_recv.at[h])


def solution(mesh):
    blocks, peers = mesh.shape["blk"], mesh.shape["uly"]

    def per_device(queries, keys, values, query_gain, key_gain, neighbors, counts):
        tokens, width = queries.shape
        hd = query_gain.shape[0]
        heads = width // hd // peers
        block = tokens * peers
        tiles = block // TILE
        vmem = pl.BlockSpec(memory_space=pltpu.VMEM)
        smem = pl.BlockSpec(memory_space=pltpu.SMEM)
        dma = pltpu.SemaphoreType.DMA
        return pl.pallas_call(
            functools.partial(kernel, blocks, peers, heads),
            out_shape=jax.ShapeDtypeStruct((tokens, width), jnp.bfloat16),
            in_specs=[smem, vmem] + [pl.BlockSpec(memory_space=pl.ANY)] * 3 + [vmem] * 2,
            out_specs=pl.BlockSpec(memory_space=pl.ANY),
            scratch_shapes=[
                pltpu.VMEM((tokens, width), jnp.bfloat16),
                pltpu.VMEM((tokens, width), jnp.bfloat16),
                pltpu.VMEM((tokens, width), jnp.bfloat16),
                pltpu.VMEM((heads, 2, (2 * REACH + 1) * block, hd), jnp.bfloat16),
                pltpu.VMEM((heads, block, hd), jnp.bfloat16),
                pltpu.VMEM((heads, peers, tokens, hd), jnp.bfloat16),
                pltpu.VMEM((heads, peers, tokens, hd), jnp.bfloat16),
                pltpu.VMEM((heads, block, 128), jnp.float32),
                pltpu.VMEM((heads, block, hd), jnp.float32),
                pltpu.VMEM((tiles, 16, SPAN), jnp.float32),
                pltpu.VMEM((heads, block, hd), jnp.bfloat16),
                pltpu.VMEM((tiles, 128), jnp.int32),
                pltpu.VMEM((tiles, 128), jnp.int32),
                pltpu.VMEM((heads, block, hd), jnp.bfloat16),
                pltpu.VMEM((heads, block, hd), jnp.bfloat16),
                pltpu.VMEM((heads, PARTS, 8, 128), jnp.float32),
                pltpu.VMEM((heads, block, hd), jnp.bfloat16),
                pltpu.VMEM((heads, PARTS, 8, 128), jnp.float32),
                dma((3,)), dma((3, heads)), dma((heads,)), dma((heads, 2, peers)),
                dma((heads, 2, 7)), dma((heads, 2, 7)),
                dma((heads, 2, 5)), dma((heads, 2, 5)),
                dma((heads,)), dma((heads,)), dma((2,)),
                dma((heads, PARTS)), dma((heads, PARTS)), dma((heads, PARTS)), dma((heads, PARTS)),
                dma((heads,)), dma((heads,)), dma((heads,)),
            ],
            compiler_params=pltpu.CompilerParams(
                collective_id=0, has_side_effects=True, vmem_limit_bytes=56 * 2 ** 20
            ),
        )(counts.reshape(1, -1), neighbors, queries, keys, values, query_gain.reshape(1, -1), key_gain.reshape(1, -1))

    tokens = P(("cfg", "blk", "uly"), None)
    return jax.shard_map(
        per_device,
        mesh=mesh,
        in_specs=(tokens, tokens, tokens, P(), P(), P("blk", None), P("blk")),
        out_specs=tokens,
        check_vma=False,
    )
```
